256 devices in a mesh: sample: 16 (over y, x), space: 16 (over z, core).
Axes of the slice: x: 4, y: 4, z: 8, core: 2. Of those that a mesh axis runs over, the one named last changes fastest.
Arguments:
- slabs: bfloat16 [16, 64, 32, 3072], P('sample', 'space'), may hold values from -6 to 6
- weight: bfloat16 [3, 3, 3, 96, 192], replicated, may hold values from -0.125 to 0.125
- cotangent: bfloat16 [16, 32, 16, 3072], P('sample', 'space'), may hold values from -6 to 6
Outputs:
- activation: bfloat16 [16, 32, 16, 3072], P('sample', 'space')
- input_grad: bfloat16 [16, 64, 32, 3072], P('sample', 'space')
- weight_grad: float32 [3, 3, 3, 96, 192], P(None, None, None, None, 'space')
The draws below stay inside these ranges and needn't reach their ends.
All inputs are finite; a program needn't handle non-finite values.
Results may differ from the reference program's by a relative error of at most 0.007.
Values may be sent and summed in bfloat16 or wider, within the bound.
A program may use at most 64 MiB of HBM per device.

```python
import jax
import jax.numpy as jnp
from jax import lax

CIN = 96
COUT = 192
DEPTH = 64
H = 32
W = 32
BATCH = 16
DOUT = 32
HOUT = 16
WOUT = 16


def spiked(array, own_key, source, target, blocks, factor):
    owner, partner = [(jnp.arange(array.shape[axis_at]) // (array.shape[axis_at] // blocks)).reshape([-1 if axis == axis_at else 1 for axis in range(array.ndim)]) for axis_at in (source, target)]
    chosen = jax.random.permutation(own_key, blocks)[partner]
    strong = (owner == chosen) | (owner == (partner + blocks // 2) % blocks)
    return jnp.where(strong, factor * array, array)


def block_scale(own_key, dims, split, smallest, high):
    def one(position, shards_of):
        draws = jax.random.uniform(jax.random.fold_in(jax.random.fold_in(own_key, 6), position), (shards_of,), jnp.float32, smallest / len(split), high / len(split))
        return jnp.repeat(jnp.exp(draws), dims[position] // shards_of).reshape((-1,) + (1,) * (len(dims) - position - 1))

    gain = one(*split[0])
    for cut in split[1:]:
        gain = gain * one(*cut)
    return gain


def normal_values(stream_key, dims, width, limit, cuts=(), dtype=jnp.bfloat16):
    entries = jax.random.normal(stream_key, dims, jnp.float32) * width
    if len(cuts) > 0:
        entries = block_scale(stream_key, dims, cuts, -0.22, 0.18) * entries
    return jnp.clip(entries, min=-limit, max=limit).astype(dtype)


def gaussian_with(stream_key, dims, spread, bound, cuts, heavy, held_as=jnp.bfloat16):
    values = spread * jax.random.normal(stream_key, dims, jnp.float32)
    if cuts:
        values = values * block_scale(stream_key, dims, cuts, -0.22, 0.18)
    return jnp.clip(spiked(values, jax.random.fold_in(stream_key, 3), *heavy), -bound, bound).astype(held_as)


def setup_inputs(seed: int = 0) -> dict:
    seeds = jax.random.split(jax.random.key(seed), 4)
    slabs = normal_values(seeds[0], (BATCH, DEPTH, H, W * CIN), 1.0, 6.0, ((0, 16), (1, 16)))
    weight = normal_values(seeds[1], (3, 3, 3, CIN, COUT), (27 * CIN) ** -0.5, 0.125)
    cotangent = gaussian_with(seeds[2], (BATCH, DOUT, HOUT, WOUT * COUT), 1.0, 6.0, ((0, 16), (1, 16)), (0, 1, 16, 2.0))
    return {"slabs": slabs, "weight": weight, "cotangent": cotangent}


layout_names = ('NDHWC', 'DHWIO', 'NDHWC')

def conv_forward(field, weight, margins):
    return lax.conv_general_dilated(field.astype(jnp.float32), weight.astype(jnp.float32), (2, 2, 2), margins, dimension_numbers=layout_names, precision=lax.Precision.HIGHEST)

def conv_input_grad(grad_pre, weight, extents, margins):
    flipped = jnp.transpose(weight[::-1, ::-1, ::-1], (0, 1, 2, 4, 3)).astype(jnp.float32)
    padding = []
    for extent, margin in zip(extents, margins):
        remain = (extent + margin[0] + margin[1] - 3) % 2
        padding.append((2 - margin[0], 2 - margin[1] + remain))
    return lax.conv_general_dilated(grad_pre.astype(jnp.float32), flipped, (1, 1, 1), padding, lhs_dilation=(2, 2, 2), dimension_numbers=layout_names, precision=lax.Precision.HIGHEST)

def weight_grad(field, grad_pre, margins):
    padded = jnp.pad(field, ((0, 0), margins[0], margins[1], margins[2], (0, 0))).astype(jnp.float32)
    grad_wide = grad_pre.astype(jnp.float32)
    out_d, out_h, out_w = (grad_pre.shape[1], grad_pre.shape[2], grad_pre.shape[3])
    collected = []
    for depth_off in range(3):
        for row_off in range(3):
            for col_off in range(3):
                window = padded[:, depth_off:depth_off + 2 * out_d - 1:2, row_off:row_off + 2 * out_h - 1:2, col_off:col_off + 2 * out_w - 1:2]
                collected.append(jnp.einsum('ndhwc,ndhwo->co', window, grad_wide, precision=lax.Precision.HIGHEST))
    return jnp.stack(collected).reshape(3, 3, 3, field.shape[-1], grad_pre.shape[-1])

def derivative(preact):
    sigmoid_val = jax.nn.sigmoid(preact)
    return sigmoid_val * (1.0 + preact * (1.0 - sigmoid_val))

def reference(slabs, weight, cotangent):
    margins = ((1, 1), (1, 1), (1, 1))

    def one_sample(running, sample_pair):
        sample_cells, sample_cot = sample_pair
        field = sample_cells.reshape(1, DEPTH, H, W, CIN)
        preact = conv_forward(field, weight, margins)
        result = jax.nn.silu(preact).astype(jnp.bfloat16)
        grad_pre = (sample_cot.reshape(preact.shape).astype(jnp.float32) * derivative(preact)).astype(jnp.bfloat16)
        grad_in = conv_input_grad(grad_pre, weight, (DEPTH, H, W), margins).astype(jnp.bfloat16)
        running = running + weight_grad(field, grad_pre, margins)
        return (running, (result.reshape(DOUT, HOUT, WOUT * COUT), grad_in.reshape(DEPTH, H, W * CIN)))
    start = jnp.zeros((3, 3, 3, CIN, COUT), jnp.float32)
    running, (activation, input_grad) = lax.scan(one_sample, start, (slabs, cotangent))
    return (activation, input_grad, running / BATCH)
```

```python
import jax
import jax.numpy as jnp
from jax import lax
from jax.sharding import PartitionSpec as P

CIN = 96
COUT = 192
DEPTH = 64
H = 32
W = 32
DOUT = 32
HOUT = 16
WOUT = 16


def from_behind(block, axis, distance):
    devices = range(lax.axis_size(axis))
    route = [(i - distance, i) for i in devices if i - distance in devices]
    return lax.ppermute(block, axis, route)


def parity_view(padded):
    count, depth_two, rows_two, cols_two, chans = padded.shape
    return padded.reshape(count, depth_two // 2, 2, rows_two // 2, 2, cols_two // 2, 2, chans)


def window_rows(parity, depth_off, row_off, col_off, out_d, out_h, out_w):
    piece = parity[
        :,
        depth_off // 2 : depth_off // 2 + out_d,
        depth_off % 2,
        row_off // 2 : row_off // 2 + out_h,
        row_off % 2,
        col_off // 2 : col_off // 2 + out_w,
        col_off % 2,
        :,
    ]
    return piece.reshape(-1, parity.shape[-1])


def conv_forward(padded, weight):
    count = padded.shape[0]
    out_d, out_h, out_w = (
        padded.shape[1] // 2 - 1,
        padded.shape[2] // 2 - 1,
        padded.shape[3] // 2 - 1,
    )
    parity = parity_view(padded)
    total = jnp.zeros((count * out_d * out_h * out_w, weight.shape[4]), jnp.float32)
    for depth_off in range(3):
        for row_off in range(3):
            for col_off in range(3):
                rows = window_rows(parity, depth_off, row_off, col_off, out_d, out_h, out_w)
                total = total + jnp.dot(
                    rows, weight[depth_off, row_off, col_off], preferred_element_type=jnp.float32
                )
    return total.reshape(count, out_d, out_h, out_w, weight.shape[4])


def kernel_terms(padded, grad_rows):
    out_d, out_h, out_w = (
        padded.shape[1] // 2 - 1,
        padded.shape[2] // 2 - 1,
        padded.shape[3] // 2 - 1,
    )
    parity = parity_view(padded)
    collected = []
    for depth_off in range(3):
        for row_off in range(3):
            for col_off in range(3):
                rows = window_rows(parity, depth_off, row_off, col_off, out_d, out_h, out_w)
                collected.append(
                    lax.dot_general(
                        rows,
                        grad_rows,
                        (((0,), (0,)), ((), ())),
                        preferred_element_type=jnp.float32,
                    )
                )
    return jnp.stack(collected).reshape(3, 3, 3, padded.shape[-1], grad_rows.shape[-1])


def padded_input_grad(grad_rows, weight, count, out_d, out_h, out_w):
    chans = weight.shape[3]
    buffers = {}
    for depth_off in range(3):
        for row_off in range(3):
            for col_off in range(3):
                term = jnp.dot(
                    grad_rows,
                    weight[depth_off, row_off, col_off].T,
                    preferred_element_type=jnp.float32,
                )
                term = term.reshape(count, out_d, out_h, out_w, chans)
                term = jnp.pad(
                    term,
                    (
                        (0, 0),
                        (depth_off // 2, 1 - depth_off // 2),
                        (row_off // 2, 1 - row_off // 2),
                        (col_off // 2, 1 - col_off // 2),
                        (0, 0),
                    ),
                )
                key_par = (depth_off % 2, row_off % 2, col_off % 2)
                if key_par in buffers:
                    buffers[key_par] = buffers[key_par] + term
                else:
                    buffers[key_par] = term
    ordered = [buffers[pd, ph, pw] for pd in range(2) for ph in range(2) for pw in range(2)]
    stacked = jnp.stack(ordered).reshape(2, 2, 2, count, out_d + 1, out_h + 1, out_w + 1, chans)
    stacked = jnp.transpose(stacked, (3, 4, 0, 5, 1, 6, 2, 7))
    return stacked.reshape(count, 2 * (out_d + 1), 2 * (out_h + 1), 2 * (out_w + 1), chans)


def derivative(preact):
    sigmoid_val = jax.nn.sigmoid(preact)
    return sigmoid_val * (1.0 + preact * (1.0 - sigmoid_val))


def per_device(slabs, weight, cotangent):
    depth_dev = slabs.shape[1]
    out_dev = depth_dev // 2
    before = from_behind(slabs[:, depth_dev - 1 :], "space", 1)
    field = jnp.concatenate([before, slabs], axis=1).reshape(1, depth_dev + 1, H, W, CIN)
    padded = jnp.pad(field, ((0, 0), (0, 1), (1, 1), (1, 1), (0, 0)))
    preact = conv_forward(padded, weight)
    result = jax.nn.silu(preact).astype(jnp.bfloat16)
    grad_pre = (cotangent.reshape(preact.shape).astype(jnp.float32) * derivative(preact)).astype(
        jnp.bfloat16
    )
    after = from_behind(grad_pre[:, :1], "space", -1)
    partial_w = kernel_terms(padded, grad_pre.reshape(-1, COUT))
    gradient = lax.psum_scatter(partial_w, "space", scatter_dimension=4, tiled=True)
    gradient = lax.psum(gradient, "sample") / lax.axis_size("sample")
    grad_ext = jnp.concatenate([grad_pre, after], axis=1).reshape(-1, COUT)
    grad_pad = padded_input_grad(grad_ext, weight, 1, out_dev + 1, HOUT, WOUT)
    grad_in = grad_pad[:, 1 : depth_dev + 1, 1 : H + 1, 1 : W + 1].astype(jnp.bfloat16)
    return (
        result.reshape(1, out_dev, HOUT, WOUT * COUT),
        grad_in.reshape(1, depth_dev, H, W * CIN),
        gradient,
    )


def solution(mesh):
    placed = (P("sample", "space", None, None), P(), P("sample", "space", None, None))
    return jax.shard_map(
        per_device,
        mesh=mesh,
        in_specs=placed,
        out_specs=(
            P("sample", "space", None, None),
            P("sample", "space", None, None),
            P(None, None, None, None, "space"),
        ),
        check_vma=False,
    )
```

```python
import functools

import jax
import jax.numpy as jnp
import numpy as np
from jax import lax
from jax.experimental import pallas as pl
from jax.experimental.pallas import tpu as pltpu
from jax.sharding import PartitionSpec as P

F32, BF16 = jnp.float32, jnp.bfloat16
MESH = pl.DeviceIdType.MESH

NY, NX, NZ = 4, 4, 8
PEERS = NY * NX
COUT = 192
LANES = 3072
PAIRS = 8
WIN = 384
HALF = COUT // 2
MINE = 12
CHUNK = 256
NT = (((1,), (1,)), ((), ()))


def dot(a, b, dims=(((1,), (0,)), ((), ()))):
    return lax.dot_general(a, b, dims, preferred_element_type=F32)


def kernel(
    x_hbm, w_hbm, cot_hbm, perm_hbm,
    act_hbm, grad_hbm, wg_hbm,
    x_in, x_halo, w_in, cot_in, perm,
    rows_f32, rows_bf, w_par, gs, part, part_bf, core_in,
    own, chunks, chunk_in, z_out, z_in, gathered, dx, act, grad, wg,
    load_sem, store_sem, halo_send, halo_recv, core_send, core_recv,
    xy_send, xy_recv, z_send, z_recv, ag_send, ag_recv,
):
    sample, space = lax.axis_index("sample"), lax.axis_index("space")
    y, x = sample // NX, sample % NX
    z, core = space // 2, space % 2
    after = {"space": (space + 1) % (2 * NZ)}
    before = {"space": (space + 2 * NZ - 1) % (2 * NZ)}
    other = {"space": z * 2 + (1 - core)}

    def plane(k):
        dy, dx_ = k // NX, k % NX
        return ((y + dy) % NY) * NX + (x + dx_) % NX

    def depth(k):
        return {"space": ((z + k) % NZ) * 2 + core}

    loads = [
        pltpu.make_async_copy(src, dst, load_sem.at[n])
        for n, (src, dst) in enumerate(
            ((x_hbm, x_in), (w_hbm, w_in), (cot_hbm, cot_in), (perm_hbm, perm))
        )
    ]
    for load in loads:
        load.start()

    barrier = pltpu.get_barrier_semaphore()
    for device in [after, before] + [depth(k) for k in range(1, NZ)] + [
        {"sample": plane(k)} for k in range(1, PEERS)
    ]:
        pl.semaphore_signal(barrier, inc=1, device_id=device, device_id_type=MESH)

    rows_f32[:, :, 0:8, :] = jnp.zeros((5, 24, 8, 128), F32)
    rows_bf[:, :, :, 0:128] = jnp.zeros((3, 5, 16, 128), BF16)

    loads[0].wait()
    pl.semaphore_wait(barrier, 2 + NZ - 1 + PEERS - 1)
    x_copy = pltpu.make_async_remote_copy(
        src_ref=x_in.at[3], dst_ref=x_halo, send_sem=halo_send.at[0], recv_sem=halo_recv.at[0],
        device_id=after, device_id_type=MESH,
    )
    x_copy.start()

    def split_rows(d, values):
        for t in range(24):
            rows_f32[d, t, 8:40] = values[:, 128 * t : 128 * t + 128].astype(F32)
        for t in range(24):
            for b in range(3):
                piece = rows_f32[d, t, pl.ds(7 + b, 16, stride=2), :]
                rows_bf[b, d, :, 128 * t + 128 : 128 * t + 256] = piece.astype(BF16)

    for d in range(4):
        split_rows(d + 1, x_in[d])

    loads[1].wait()
    w_par[...] = jnp.zeros(w_par.shape, BF16)
    w_par[0, :, 32:320, 0:COUT] = w_in[...]
    w_par[1, :, 96:384, 0:COUT] = w_in[...]
    chunks[PEERS - 3 :] = jnp.zeros((3, HALF, CHUNK), BF16)
    own[PEERS - 3 :] = jnp.zeros((3, HALF, CHUNK), F32)

    def windows(par, a, b):
        return jnp.concatenate(
            [
                rows_bf[b, a + 2 * i, :, 384 * m + 128 * par : 384 * m + 128 * par + WIN]
                for i in range(2)
                for m in range(PAIRS)
            ],
            axis=0,
        )

    pre = [None, None]
    for a in (1, 2, 0):
        if a == 0:
            x_copy.wait()
            halo = x_halo[...]
            split_rows(0, jnp.where(space == 0, jnp.zeros_like(halo), halo))
        for par in range(2):
            for b in range(3):
                term = dot(windows(par, a, b), w_par[par, 3 * a + b])
                pre[par] = term if pre[par] is None else pre[par] + term

    loads[2].wait()
    activation = []
    for par in range(2):
        cot = jnp.concatenate(
            [
                cot_in[i, :, 384 * m + 128 * par : 384 * m + 128 * par + 256]
                for i in range(2)
                for m in range(PAIRS)
            ],
            axis=0,
        ).astype(F32)
        if par == 1:
            cot = pltpu.roll(cot, 192, 1)
        sigmoid_val = jax.nn.sigmoid(pre[par])
        activation.append(pre[par] * sigmoid_val)
        g = cot * (sigmoid_val * (1.0 + pre[par] * (1.0 - sigmoid_val)))
        g = g.astype(BF16)
        for i in range(2):
            gs[i, par] = g[128 * i : 128 * i + 128]
    g_copy = pltpu.make_async_remote_copy(
        src_ref=gs.at[0], dst_ref=gs.at[2], send_sem=halo_send.at[1], recv_sem=halo_recv.at[1],
        device_id=before, device_id_type=MESH,
    )
    g_copy.start()

    loads[3].wait()
    turned = [
        dot(perm[...], jnp.concatenate([gs[0, par], gs[1, par]], axis=0), NT).astype(BF16)
        for par in range(2)
    ]
    core_copies = []
    for tap in range(9):
        lanes = pl.ds(WIN * tap, WIN)
        total = dot(turned[0], windows(0, tap // 3, tap % 3)) + pltpu.roll(
            dot(turned[1], windows(1, tap // 3, tap % 3)), WIN - 64, 1
        )
        part[:, lanes] = total
        part_bf[:, lanes] = total.astype(BF16)
        copy = pltpu.make_async_remote_copy(
            src_ref=part_bf.at[pl.ds(pl.multiple_of((1 - core) * HALF, HALF), HALF), lanes],
            dst_ref=core_in.at[:, lanes],
            send_sem=core_send.at[tap], recv_sem=core_recv.at[tap],
            device_id=other, device_id_type=MESH,
        )
        copy.start()
        core_copies.append(copy)

    mine = pl.ds(pl.multiple_of(core * HALF, HALF), HALF)
    for tap in range(9):
        core_copies[tap].wait()
        lanes = pl.ds(WIN * tap, WIN)
        total = part[mine, lanes] + core_in[:, lanes].astype(F32)
        for u in range(3):
            t = 3 * tap + u
            piece = total[:, 128 * u : 128 * u + 128]
            own[t // 2, :, 128 * (t % 2) : 128 * (t % 2) + 128] = piece
            chunks[t // 2, :, 128 * (t % 2) : 128 * (t % 2) + 128] = piece.astype(BF16)

    xy_copies = []
    for k in range(1, PEERS):
        copy = pltpu.make_async_remote_copy(
            src_ref=chunks.at[plane(k)], dst_ref=chunk_in.at[k - 1],
            send_sem=xy_send.at[k - 1], recv_sem=xy_recv.at[k - 1],
            device_id={"sample": plane(k)}, device_id_type=MESH,
        )
        copy.start()
        xy_copies.append(copy)

    low = lax.broadcasted_iota(jnp.int32, (256, 128), 1) < 64
    moved = pltpu.roll(activation[1], 64, 1)
    middle = jnp.where(low, activation[0][:, 128:], moved[:, :128])
    dense = jnp.concatenate([activation[0][:, :128], middle, moved[:, 128:]], axis=1).astype(BF16)
    for i in range(2):
        for m in range(PAIRS):
            row = 128 * i + 16 * m
            act[i, :, 384 * m : 384 * m + 384] = dense[row : row + 16]
    act_store = pltpu.make_async_copy(act, act_hbm, store_sem.at[0])
    act_store.start()

    row = lax.broadcasted_iota(jnp.int32, (128, 256), 0)
    last_row = row % 16 == 15

    def shifted(value):
        up = pltpu.roll(value.astype(F32), 127, 0)
        return jnp.where(last_row, 0.0, up).astype(BF16)

    g_copy.wait()
    g_rows = [[gs[i, par] for par in range(2)] for i in range(3)]
    outside = space == 2 * NZ - 1
    for par in range(2):
        g_rows[2][par] = jnp.where(outside, jnp.zeros_like(g_rows[2][par]), g_rows[2][par])
    g_shift = [[shifted(g_rows[i][par]) for par in range(2)] for i in range(3)]

    def terms(par, first, row_par, a):
        def both(source):
            return jnp.concatenate([source[first][par], source[first + 1][par]], axis=0)

        if row_par == 0:
            return dot(both(g_rows), w_par[par, 3 * a + 1], NT)
        return dot(both(g_rows), w_par[par, 3 * a + 2], NT) + dot(
            both(g_shift), w_par[par, 3 * a], NT
        )

    for depth_par in range(2):
        for row_par in range(2):
            sums = []
            for par in range(2):
                if depth_par == 0:
                    sums.append(terms(par, 0, row_par, 1))
                else:
                    sums.append(terms(par, 0, row_par, 2) + terms(par, 1, row_par, 0))
            for i in range(2):
                for m in range(PAIRS):
                    at = 128 * i + 16 * m
                    value = sums[1][at : at + 16]
                    left = sums[0][at : at + 16, 128:]
                    if m < PAIRS - 1:
                        right = sums[0][at + 16 : at + 32, :128]
                    else:
                        right = jnp.zeros((16, 128), F32)
                    value = value + jnp.concatenate([left, right], axis=1)
                    for u in range(3):
                        piece = value[:, 128 * u : 128 * u + 128]
                        dx[2 * i + depth_par, 3 * m + u, pl.ds(row_par, 16, stride=2), :] = piece
    for d in range(4):
        for t in range(24):
            grad[d, :, 128 * t : 128 * t + 128] = dx[d, t].astype(BF16)
    grad_store = pltpu.make_async_copy(grad, grad_hbm, store_sem.at[1])
    grad_store.start()

    for copy in xy_copies:
        copy.wait()
    total = own[sample]
    for k in range(PEERS - 1):
        total = total + chunk_in[k].astype(F32)
    for k in range(NZ):
        z_out[k, 0:MINE] = total[MINE * k : MINE * k + MINE]
        z_out[k, MINE:16] = jnp.zeros((16 - MINE, CHUNK), F32)

    z_copies = []
    for k in range(1, NZ):
        copy = pltpu.make_async_remote_copy(
            src_ref=z_out.at[(z + k) % NZ], dst_ref=z_in.at[k - 1],
            send_sem=z_send.at[k - 1], recv_sem=z_recv.at[k - 1],
            device_id=depth(k), device_id_type=MESH,
        )
        copy.start()
        z_copies.append(copy)
    for copy in z_copies:
        copy.wait()
    total = z_out[z]
    for k in range(NZ - 1):
        total = total + z_in[k]
    gathered[sample] = total * (1.0 / PEERS)

    ag_copies = []
    for k in range(1, PEERS):
        copy = pltpu.make_async_remote_copy(
            src_ref=gathered.at[sample], dst_ref=gathered.at[sample],
            send_sem=ag_send.at[k - 1], recv_sem=ag_recv.at[k - 1],
            device_id={"sample": plane(k)}, device_id_type=MESH,
        )
        copy.start()
        ag_copies.append(copy)
    for copy in ag_copies:
        copy.wait()
    for tap in range(9):
        window = jnp.concatenate(
            [
                gathered[t // 2, :, 128 * (t % 2) : 128 * (t % 2) + 128]
                for t in range(3 * tap, 3 * tap + 3)
            ],
            axis=1,
        )
        for e in range(3):
            wg[3 * tap + e] = window[0:MINE, 32 + 96 * e : 128 + 96 * e]
    wg_store = pltpu.make_async_copy(wg, wg_hbm, store_sem.at[2])
    wg_store.start()
    act_store.wait()
    grad_store.wait()
    wg_store.wait()


def channel_order():
    table = np.zeros((COUT, 256), np.float32)
    for r in range(COUT):
        c, rest = divmod(r, HALF)
        zz, t = divmod(rest, MINE)
        table[r, (2 * zz + c) * MINE + t] = 1.0
    return jnp.asarray(table, BF16)


def per_device(slabs, weight, cotangent):
    any_space = pl.BlockSpec(memory_space=pl.ANY)
    dma = pltpu.SemaphoreType.DMA
    activation, input_grad, gradient = pl.pallas_call(
        kernel,
        out_shape=(
            jax.ShapeDtypeStruct((2, 16, LANES), BF16),
            jax.ShapeDtypeStruct((4, 32, LANES), BF16),
            jax.ShapeDtypeStruct((27, MINE, 96), F32),
        ),
        in_specs=[any_space] * 4,
        out_specs=(any_space,) * 3,
        scratch_shapes=[
            pltpu.VMEM((4, 32, LANES), BF16),
            pltpu.VMEM((32, LANES), BF16),
            pltpu.VMEM((9, 288, COUT), BF16),
            pltpu.VMEM((2, 16, LANES), BF16),
            pltpu.VMEM((COUT, 256), BF16),
            pltpu.VMEM((5, 24, 40, 128), F32),
            pltpu.VMEM((3, 5, 16, LANES + 128), BF16),
            pltpu.VMEM((2, 9, WIN, 256), BF16),
            pltpu.VMEM((3, 2, 128, 256), BF16),
            pltpu.VMEM((COUT, 9 * WIN), F32),
            pltpu.VMEM((COUT, 9 * WIN), BF16),
            pltpu.VMEM((HALF, 9 * WIN), BF16),
            pltpu.VMEM((PEERS, HALF, CHUNK), F32),
            pltpu.VMEM((PEERS, HALF, CHUNK), BF16),
            pltpu.VMEM((PEERS - 1, HALF, CHUNK), BF16),
            pltpu.VMEM((NZ, 16, CHUNK), F32),
            pltpu.VMEM((NZ - 1, 16, CHUNK), F32),
            pltpu.VMEM((PEERS, 16, CHUNK), F32),
            pltpu.VMEM((4, 24, 32, 128), F32),
            pltpu.VMEM((2, 16, LANES), BF16),
            pltpu.VMEM((4, 32, LANES), BF16),
            pltpu.VMEM((27, MINE, 96), F32),
            dma((4,)), dma((3,)), dma((2,)), dma((2,)), dma((9,)), dma((9,)),
            dma((PEERS - 1,)), dma((PEERS - 1,)), dma((NZ - 1,)), dma((NZ - 1,)),
            dma((PEERS - 1,)), dma((PEERS - 1,)),
        ],
        compiler_params=pltpu.CompilerParams(
            collective_id=0, has_side_effects=True, vmem_limit_bytes=60 << 20
        ),
        name="conv_layer",
    )(
        slabs.reshape(4, 32, LANES),
        weight.reshape(9, 288, COUT),
        cotangent.reshape(2, 16, LANES),
        channel_order(),
    )
    return (
        activation.reshape(1, 2, 16, LANES),
        input_grad.reshape(1, 4, 32, LANES),
        jnp.swapaxes(gradient, 1, 2).reshape(3, 3, 3, 96, MINE),
    )


def solution(mesh):
    placed = (P("sample", "space", None, None), P(), P("sample", "space", None, None))
    return jax.shard_map(
        per_device,
        mesh=mesh,
        in_specs=placed,
        out_specs=(
            P("sample", "space", None, None),
            P("sample", "space", None, None),
            P(None, None, None, None, "space"),
        ),
        check_vma=False,
    )
```

```python
import functools

import jax
import jax.numpy as jnp
import numpy as np
from jax import lax
from jax.experimental import pallas as pl
from jax.experimental.pallas import tpu as pltpu
from jax.sharding import PartitionSpec as P

F32, BF16 = jnp.float32, jnp.bfloat16
MESH = pl.DeviceIdType.MESH

NY, NX, NZ = 4, 4, 8
PEERS = NY * NX
COUT = 192
LANES = 3072
PAIRS = 8
WIN = 384
HALF = COUT // 2
MINE = 12
TILES = 21
UNITS = 8
NT = (((1,), (1,)), ((), ()))


def dot(a, b, dims=(((1,), (0,)), ((), ()))):
    return lax.dot_general(a, b, dims, preferred_element_type=F32)


def kernel(
    x_hbm, w_hbm, cot_hbm, perm_hbm,
    act, grad, wg,
    x_in, x_halo, w_in, cot_in, perm,
    rows_f32, rows_bf, w_par, gs, part, part_bf, core_in,
    own, chunks, chunk_in, summed, z_out, z_in, gathered, dx,
    load_sem, halo_send, halo_recv, core_send, core_recv,
    xy_send, xy_recv, z_send, z_recv, ag_send, ag_recv,
):
    sample, space = lax.axis_index("sample"), lax.axis_index("space")
    y, x = sample // NX, sample % NX
    z, core = space // 2, space % 2
    after = {"space": (space + 1) % (2 * NZ)}
    before = {"space": (space + 2 * NZ - 1) % (2 * NZ)}
    other = {"space": z * 2 + (1 - core)}

    def plane(k):
        dy, dx_ = k // NX, k % NX
        return ((y + dy) % NY) * NX + (x + dx_) % NX

    def depth(k):
        return {"space": ((z + k) % NZ) * 2 + core}

    loads = [
        pltpu.make_async_copy(src, dst, load_sem.at[n])
        for n, (src, dst) in enumerate(
            ((x_hbm, x_in), (w_hbm, w_in), (cot_hbm, cot_in), (perm_hbm, perm))
        )
    ]
    for load in loads:
        load.start()

    barrier = pltpu.get_barrier_semaphore()
    for device in [after, before] + [depth(k) for k in range(1, NZ)] + [
        {"sample": plane(k)} for k in range(1, PEERS)
    ]:
        pl.semaphore_signal(barrier, inc=1, device_id=device, device_id_type=MESH)

    rows_f32[:, :, 0:8, :] = jnp.zeros((5, 24, 8, 128), F32)
    rows_bf[:, :, :, 0:128] = jnp.zeros((3, 5, 16, 128), BF16)

    loads[0].wait()
    pl.semaphore_wait(barrier, 2 + NZ - 1 + PEERS - 1)
    x_copy = pltpu.make_async_remote_copy(
        src_ref=x_in.at[3], dst_ref=x_halo, send_sem=halo_send.at[0], recv_sem=halo_recv.at[0],
        device_id=after, device_id_type=MESH,
    )
    x_copy.start()

    def split_rows(d, values):
        for t in range(24):
            rows_f32[d, t, 8:40] = values[:, 128 * t : 128 * t + 128].astype(F32)
        for t in range(24):
            for b in range(3):
                piece = rows_f32[d, t, pl.ds(7 + b, 16, stride=2), :]
                rows_bf[b, d, :, 128 * t + 128 : 128 * t + 256] = piece.astype(BF16)

    for d in range(4):
        split_rows(d + 1, x_in[d])

    loads[1].wait()
    w_par[...] = jnp.zeros(w_par.shape, BF16)
    w_par[0, :, 32:320, 0:COUT] = w_in[...]
    w_par[1, :, 96:384, 0:COUT] = w_in[...]
    chunks[PEERS - 1, 96:128] = jnp.zeros((32, 128), BF16)
    own[PEERS - 1, 96:128] = jnp.zeros((32, 128), F32)

    def windows(par, a, b):
        return jnp.concatenate(
            [
                rows_bf[b, a + 2 * i, :, 384 * m + 128 * par : 384 * m + 128 * par + WIN]
                for i in range(2)
                for m in range(PAIRS)
            ],
            axis=0,
        )

    pre = [None, None]
    for a in (1, 2, 0):
        if a == 0:
            x_copy.wait()
            halo = x_halo[...]
            split_rows(0, jnp.where(space == 0, jnp.zeros_like(halo), halo))
        for par in range(2):
            for b in range(3):
                term = dot(windows(par, a, b), w_par[par, 3 * a + b])
                pre[par] = term if pre[par] is None else pre[par] + term

    loads[2].wait()
    activation = []
    for par in range(2):
        cot = jnp.concatenate(
            [
                cot_in[i, :, 384 * m + 128 * par : 384 * m + 128 * par + 256]
                for i in range(2)
                for m in range(PAIRS)
            ],
            axis=0,
        ).astype(F32)
        if par == 1:
            cot = pltpu.roll(cot, 192, 1)
        sigmoid_val = jax.nn.sigmoid(pre[par])
        activation.append(pre[par] * sigmoid_val)
        g = cot * (sigmoid_val * (1.0 + pre[par] * (1.0 - sigmoid_val)))
        g = g.astype(BF16)
        for i in range(2):
            gs[i, par] = g[128 * i : 128 * i + 128]
    g_copy = pltpu.make_async_remote_copy(
        src_ref=gs.at[0], dst_ref=gs.at[2], send_sem=halo_send.at[1], recv_sem=halo_recv.at[1],
        device_id=before, device_id_type=MESH,
    )
    g_copy.start()

    loads[3].wait()
    turned = [
        dot(perm[...], jnp.concatenate([gs[0, par], gs[1, par]], axis=0), NT).astype(BF16)
        for par in range(2)
    ]
    core_copies = []
    for tap in range(9):
        lanes = pl.ds(WIN * tap, WIN)
        total = dot(turned[0], windows(0, tap // 3, tap % 3)) + pltpu.roll(
            dot(turned[1], windows(1, tap // 3, tap % 3)), WIN - 64, 1
        )
        part[:, lanes] = total
        part_bf[:, lanes] = total.astype(BF16)
        copy = pltpu.make_async_remote_copy(
            src_ref=part_bf.at[pl.ds(pl.multiple_of((1 - core) * HALF, HALF), HALF), lanes],
            dst_ref=core_in.at[:, lanes],
            send_sem=core_send.at[tap], recv_sem=core_recv.at[tap],
            device_id=other, device_id_type=MESH,
        )
        copy.start()
        core_copies.append(copy)

    mine = pl.ds(pl.multiple_of(core * HALF, HALF), HALF)

    def place(tile, value):
        for block in range(6):
            unit = 6 * tile + block
            at = 16 * (unit % UNITS)
            own[unit // UNITS, at : at + 16] = value[16 * block : 16 * block + 16]
            chunks[unit // UNITS, at : at + 16] = value[16 * block : 16 * block + 16].astype(BF16)

    quarter = lax.broadcasted_iota(jnp.int32, (HALF, 128), 1) // 32
    shared = None
    for tap in range(9):
        core_copies[tap].wait()
        lanes = pl.ds(WIN * tap, WIN)
        total = part[mine, lanes] + core_in[:, lanes].astype(F32)
        total = pltpu.roll(total, WIN - 32, 1)
        place(2 * tap, total[:, 0:128])
        place(2 * tap + 1, total[:, 128:256])
        rest = total[:, 256:384]
        if tap % 4 == 0:
            shared = rest
        else:
            shared = jnp.where(quarter == tap % 4, pltpu.roll(rest, 32 * (tap % 4), 1), shared)
        if tap % 4 == 3 or tap == 8:
            place(18 + tap // 4, shared)

    xy_copies = []
    for k in range(1, PEERS):
        copy = pltpu.make_async_remote_copy(
            src_ref=chunks.at[plane(k)], dst_ref=chunk_in.at[k - 1],
            send_sem=xy_send.at[k - 1], recv_sem=xy_recv.at[k - 1],
            device_id={"sample": plane(k)}, device_id_type=MESH,
        )
        copy.start()
        xy_copies.append(copy)

    low = lax.broadcasted_iota(jnp.int32, (256, 128), 1) < 64
    moved = pltpu.roll(activation[1], 64, 1)
    middle = jnp.where(low, activation[0][:, 128:], moved[:, :128])
    dense = jnp.concatenate([activation[0][:, :128], middle, moved[:, 128:]], axis=1).astype(BF16)
    for i in range(2):
        for m in range(PAIRS):
            row = 128 * i + 16 * m
            act[i, :, 384 * m : 384 * m + 384] = dense[row : row + 16]

    row = lax.broadcasted_iota(jnp.int32, (128, 256), 0)
    last_row = row % 16 == 15

    def shifted(value):
        up = pltpu.roll(value.astype(F32), 127, 0)
        return jnp.where(last_row, 0.0, up).astype(BF16)

    g_copy.wait()
    g_rows = [[gs[i, par] for par in range(2)] for i in range(3)]
    outside = space == 2 * NZ - 1
    for par in range(2):
        g_rows[2][par] = jnp.where(outside, jnp.zeros_like(g_rows[2][par]), g_rows[2][par])
    g_shift = [[shifted(g_rows[i][par]) for par in range(2)] for i in range(3)]

    def terms(par, first, row_par, a):
        def both(source):
            return jnp.concatenate([source[first][par], source[first + 1][par]], axis=0)

        if row_par == 0:
            return dot(both(g_rows), w_par[par, 3 * a + 1], NT)
        return dot(both(g_rows), w_par[par, 3 * a + 2], NT) + dot(
            both(g_shift), w_par[par, 3 * a], NT
        )

    for depth_par in range(2):
        for row_par in range(2):
            sums = []
            for par in range(2):
                if depth_par == 0:
                    sums.append(terms(par, 0, row_par, 1))
                else:
                    sums.append(terms(par, 0, row_par, 2) + terms(par, 1, row_par, 0))
            for i in range(2):
                for m in range(PAIRS):
                    at = 128 * i + 16 * m
                    value = sums[1][at : at + 16]
                    left = sums[0][at : at + 16, 128:]
                    if m < PAIRS - 1:
                        right = sums[0][at + 16 : at + 32, :128]
                    else:
                        right = jnp.zeros((16, 128), F32)
                    value = value + jnp.concatenate([left, right], axis=1)
                    for u in range(3):
                        piece = value[:, 128 * u : 128 * u + 128]
                        dx[2 * i + depth_par, 3 * m + u, pl.ds(row_par, 16, stride=2), :] = piece
    for d in range(4):
        for t in range(24):
            grad[d, :, 128 * t : 128 * t + 128] = dx[d, t].astype(BF16)

    for copy in xy_copies:
        copy.wait()
    total = own[sample]
    for k in range(PEERS - 1):
        total = total + chunk_in[k].astype(F32)
    summed[...] = total
    for k in range(NZ):
        for t in range(2):
            z_out[k, pl.ds(t, 8, stride=2), :] = summed[pl.ds(2 * k + t, 8, stride=16), :]

    z_copies = []
    for k in range(1, NZ):
        copy = pltpu.make_async_remote_copy(
            src_ref=z_out.at[(z + k) % NZ], dst_ref=z_in.at[k - 1],
            send_sem=z_send.at[k - 1], recv_sem=z_recv.at[k - 1],
            device_id=depth(k), device_id_type=MESH,
        )
        copy.start()
        z_copies.append(copy)
    for copy in z_copies:
        copy.wait()
    total = z_out[z]
    for k in range(NZ - 1):
        total = total + z_in[k]
    gathered[sample] = total * (1.0 / PEERS)

    ag_copies = []
    for k in range(1, PEERS):
        copy = pltpu.make_async_remote_copy(
            src_ref=gathered.at[sample], dst_ref=gathered.at[sample],
            send_sem=ag_send.at[k - 1], recv_sem=ag_recv.at[k - 1],
            device_id={"sample": plane(k)}, device_id_type=MESH,
        )
        copy.start()
        ag_copies.append(copy)
    for copy in ag_copies:
        copy.wait()
    rows = gathered[...].reshape(16 * PEERS, 128)

    def tile_rows(tile):
        return rows[MINE * tile : MINE * tile + MINE]

    for tap in range(9):
        rest = tile_rows(18 + tap // 4)[:, 32 * (tap % 4) : 32 * (tap % 4) + 32]
        window = jnp.concatenate([tile_rows(2 * tap), tile_rows(2 * tap + 1), rest], axis=1)
        for e in range(3):
            wg[3 * tap + e] = window[:, 96 * e : 96 * e + 96]


def hand_over(*refs):
    count = len(refs) // 2
    sems = refs[-1]
    copies = [
        pltpu.make_async_copy(refs[n], refs[count + n], sems.at[n]) for n in range(count)
    ]
    for copy in copies:
        copy.start()
    for copy in copies:
        copy.wait()


def channel_order():
    table = np.zeros((COUT, 256), np.float32)
    for r in range(COUT):
        c, rest = divmod(r, HALF)
        block, inside = divmod(rest, 16)
        zz, t = divmod(inside, 2)
        table[r, (2 * zz + c) * MINE + 2 * block + t] = 1.0
    return jnp.asarray(table, BF16)


def per_device(slabs, weight, cotangent):
    any_space = pl.BlockSpec(memory_space=pl.ANY)
    dma = pltpu.SemaphoreType.DMA
    shapes = (((2, 16, LANES), BF16), ((4, 32, LANES), BF16), ((27, MINE, 96), F32))
    on_chip = pl.BlockSpec(memory_space=pltpu.VMEM)
    results = pl.pallas_call(
        kernel,
        out_shape=tuple(pltpu.VMEM(*shape) for shape in shapes),
        in_specs=[pl.BlockSpec(memory_space=pltpu.HBM)] * 4,
        out_specs=(on_chip,) * 3,
        scratch_shapes=[
            pltpu.VMEM((4, 32, LANES), BF16),
            pltpu.VMEM((32, LANES), BF16),
            pltpu.VMEM((9, 288, COUT), BF16),
            pltpu.VMEM((2, 16, LANES), BF16),
            pltpu.VMEM((COUT, 256), BF16),
            pltpu.VMEM((5, 24, 40, 128), F32),
            pltpu.VMEM((3, 5, 16, LANES + 128), BF16),
            pltpu.VMEM((2, 9, WIN, 256), BF16),
            pltpu.VMEM((3, 2, 128, 256), BF16),
            pltpu.VMEM((COUT, 9 * WIN), F32),
            pltpu.VMEM((COUT, 9 * WIN), BF16),
            pltpu.VMEM((HALF, 9 * WIN), BF16),
            pltpu.VMEM((PEERS, 128, 128), F32),
            pltpu.VMEM((PEERS, 128, 128), BF16),
            pltpu.VMEM((PEERS - 1, 128, 128), BF16),
            pltpu.VMEM((128, 128), F32),
            pltpu.VMEM((NZ, 16, 128), F32),
            pltpu.VMEM((NZ - 1, 16, 128), F32),
            pltpu.VMEM((PEERS, 16, 128), F32),
            pltpu.VMEM((4, 24, 32, 128), F32),
            dma((4,)), dma((2,)), dma((2,)), dma((9,)), dma((9,)),
            dma((PEERS - 1,)), dma((PEERS - 1,)), dma((NZ - 1,)), dma((NZ - 1,)),
            dma((PEERS - 1,)), dma((PEERS - 1,)),
        ],
        compiler_params=pltpu.CompilerParams(
            collective_id=0, has_side_effects=True, vmem_limit_bytes=48 << 20
        ),
        name="conv_layer",
    )(
        *(
            pltpu.with_memory_space_constraint(array, pltpu.HBM)
            for array in (
                slabs.reshape(4, 32, LANES),
                weight.reshape(9, 288, COUT),
                cotangent.reshape(2, 16, LANES),
                channel_order(),
            )
        )
    )
    activation, input_grad, gradient = pl.pallas_call(
        hand_over,
        out_shape=tuple(jax.ShapeDtypeStruct(*shape) for shape in shapes),
        in_specs=[on_chip] * 3,
        out_specs=(any_space,) * 3,
        scratch_shapes=[dma((3,))],
        compiler_params=pltpu.CompilerParams(vmem_limit_bytes=4 << 20),
        name="hand_over",
    )(*(pltpu.with_memory_space_constraint(array, pltpu.VMEM) for array in results))
    return (
        activation.reshape(1, 2, 16, LANES),
        input_grad.reshape(1, 4, 32, LANES),
        jnp.swapaxes(gradient, 1, 2).reshape(3, 3, 3, 96, MINE),
    )


def solution(mesh):
    placed = (P("sample", "space", None, None), P(), P("sample", "space", None, None))
    return jax.shard_map(
        per_device,
        mesh=mesh,
        in_specs=placed,
        out_specs=(
            P("sample", "space", None, None),
            P("sample", "space", None, None),
            P(None, None, None, None, "space"),
        ),
        check_vma=False,
    )
```

```python
import functools

import jax
import jax.numpy as jnp
import numpy as np
from jax import lax
from jax.experimental import pallas as pl
from jax.experimental.pallas import tpu as pltpu
from jax.sharding import PartitionSpec as P

F32, BF16 = jnp.float32, jnp.bfloat16
MESH = pl.DeviceIdType.MESH

NY, NX, NZ = 4, 4, 8
PEERS = NY * NX
COUT = 192
LANES = 3072
PAIRS = 8
WIN = 384
HALF = COUT // 2
MINE = 12
TILES = 21
UNITS = 8
BLOCKS = UNITS * PEERS
NT = (((1,), (1,)), ((), ()))


def dot(a, b, dims=(((1,), (0,)), ((), ()))):
    return lax.dot_general(a, b, dims, preferred_element_type=F32)


def position():
    sample, space = lax.axis_index("sample"), lax.axis_index("space")
    after = {"space": (space + 1) % (2 * NZ)}
    before = {"space": (space + 2 * NZ - 1) % (2 * NZ)}
    return sample, space, after, before


def greet(barrier, device, exists=None):
    def signal():
        pl.semaphore_signal(barrier, inc=1, device_id=device, device_id_type=MESH)

    if exists is None:
        signal()
    else:
        pl.when(exists)(signal)


def split_rows(values, rows_f32, rows_bf, rows_sh, d):
    for t in range(24):
        rows_f32[t, 8:40] = values[:, 128 * t : 128 * t + 128].astype(F32)
    lane = lax.broadcasted_iota(jnp.int32, (16, 128), 1)
    zero = jnp.zeros((16, 128), F32)
    for b in range(3):
        pieces = [rows_f32[t, pl.ds(7 + b, 16, stride=2), :] for t in range(24)]
        for t in range(24):
            rows_bf[b, d, :, 128 * t + 128 : 128 * t + 256] = pieces[t].astype(BF16)
        for n, left in enumerate((32, 96)):
            rolled = [pltpu.roll(piece, 128 - left, 1) for piece in pieces]
            for t in range(25):
                low = rolled[t - 1] if t > 0 else zero
                high = rolled[t] if t < 24 else zero
                piece = jnp.where(lane < 128 - left, low, high)
                rows_sh[n, b, d, :, 128 * t : 128 * t + 128] = piece.astype(BF16)


def windows(rows_bf, par, d, b):
    return jnp.concatenate(
        [
            rows_bf[b, d, :, 384 * m + 128 * par : 384 * m + 128 * par + WIN]
            for m in range(PAIRS)
        ],
        axis=0,
    )


def aligned_windows(rows_sh, d, b):
    return jnp.concatenate(
        [windows(rows_sh.at[par], par, d, b) for par in range(2)], axis=0
    )


def cotangent_rows(cot_in, i, par):
    cot = jnp.concatenate(
        [
            cot_in[i, :, 384 * m + 128 * par : 384 * m + 128 * par + 256]
            for m in range(PAIRS)
        ],
        axis=0,
    ).astype(F32)
    return pltpu.roll(cot, 192, 1) if par == 1 else cot


def pointwise(pre, cot):
    sigmoid_val = jax.nn.sigmoid(pre)
    g = cot * (sigmoid_val * (1.0 + pre * (1.0 - sigmoid_val)))
    return pre * sigmoid_val, g.astype(BF16)


def side_by_side(even, odd, out):
    low = lax.broadcasted_iota(jnp.int32, (128, 128), 1) < 64
    moved = pltpu.roll(odd, 64, 1)
    middle = jnp.where(low, even[:, 128:], moved[:, :128])
    dense = jnp.concatenate([even[:, :128], middle, moved[:, 128:]], axis=1).astype(BF16)
    for m in range(PAIRS):
        out[:, 384 * m : 384 * m + 384] = dense[16 * m : 16 * m + 16]


def turn(perm, g):
    return jnp.concatenate([dot(perm[...], g[par], NT).astype(BF16) for par in range(2)], axis=1)


def first_kernel(
    x_hbm, w_hbm, cot_hbm, perm_hbm,
    x_halo, cot_in, perm, rows_sh, w_par, pre0, g1, part1, act1,
    x_in, w_in, rows_f32, rows_bf, load_sem, halo_send, halo_recv,
):
    _, space, after, before = position()
    has_before, has_after = space > 0, space < 2 * NZ - 1
    neighbours = 2 - jnp.where(has_before, 0, 1) - jnp.where(has_after, 0, 1)
    loads = [
        pltpu.make_async_copy(src, dst, load_sem.at[n])
        for n, (src, dst) in enumerate(
            ((x_hbm, x_in), (w_hbm, w_in), (cot_hbm, cot_in), (perm_hbm, perm))
        )
    ]
    for load in loads:
        load.start()
    barrier = pltpu.get_barrier_semaphore()
    @pl.when(jnp.logical_not(has_before))
    def _():
        x_halo[...] = jnp.zeros_like(x_halo)

    greet(barrier, after, has_after)
    greet(barrier, before, has_before)

    rows_f32[:, :, 0:8, :] = jnp.zeros((4, 24, 8, 128), F32)
    rows_bf[:, :, :, 0:128] = jnp.zeros((3, 5, 16, 128), BF16)
    loads[0].wait()
    pl.semaphore_wait(barrier, neighbours)
    x_copy = pltpu.make_async_remote_copy(
        src_ref=x_in.at[3], dst_ref=x_halo, send_sem=halo_send, recv_sem=halo_recv,
        device_id=after, device_id_type=MESH,
    )
    pl.when(has_after)(x_copy.start)
    for d in range(4):
        split_rows(x_in[d], rows_f32.at[d], rows_bf, rows_sh, d + 1)
    w_par[:, :, :, 128:] = jnp.zeros((2, 9, WIN, 128), BF16)
    w_par[0, :, 0:32, 0:128] = jnp.zeros((9, 32, 128), BF16)
    w_par[0, :, 320:, 0:128] = jnp.zeros((9, 64, 128), BF16)
    w_par[1, :, 0:96, 0:128] = jnp.zeros((9, 96, 128), BF16)
    loads[1].wait()
    w_par[0, :, 32:320, 0:COUT] = w_in[...]
    w_par[1, :, 96:384, 0:COUT] = w_in[...]

    pre1 = []
    for par in range(2):
        total0, total1 = None, None
        for tap in range(9):
            a, b = tap // 3, tap % 3
            high = windows(rows_bf, par, a + 2, b)
            if a == 0:
                term1 = dot(high, w_par[par, tap])
            else:
                both = dot(
                    jnp.concatenate([windows(rows_bf, par, a, b), high], axis=0), w_par[par, tap]
                )
                term1 = both[128:]
                total0 = both[:128] if total0 is None else total0 + both[:128]
            total1 = term1 if total1 is None else total1 + term1
        pre0[par] = total0
        pre1.append(total1)
    loads[2].wait()
    acts = []
    for par in range(2):
        value, g = pointwise(pre1[par], cotangent_rows(cot_in, 1, par))
        acts.append(value)
        g1[par] = g
    side_by_side(acts[0], acts[1], act1)
    loads[3].wait()
    turned = turn(perm, g1)
    for tap in range(9):
        part1[:, WIN * tap : WIN * tap + WIN] = dot(
            turned, aligned_windows(rows_sh, tap // 3 + 2, tap % 3)
        )
    pl.when(has_after)(x_copy.wait_send)
    pl.when(has_before)(x_copy.wait_recv)


def second_kernel(
    x_halo, cot_in, perm, rows_sh_in, w_par, pre0, g1, part1,
    act0, grad, wg,
    rows_f32, rows_bf, rows_sh, g0, g2, part, part_bf, core_in,
    own, chunks, chunk_in, summed, z_out, z_in, gathered, dx,
    halo_send, halo_recv, core_send, core_recv,
    xy_send, xy_recv, z_send, z_recv, ag_send, ag_recv,
):
    sample, space, after, before = position()
    has_before, has_after = space > 0, space < 2 * NZ - 1
    neighbours = 2 - jnp.where(has_before, 0, 1) - jnp.where(has_after, 0, 1)
    y, x = sample // NX, sample % NX
    z, core = space // 2, space % 2
    other = {"space": z * 2 + (1 - core)}

    def plane(k):
        return ((y + k // NX) % NY) * NX + (x + k % NX) % NX

    def depth(k):
        return {"space": ((z + k) % NZ) * 2 + core}

    def hops(k):
        return min(k // NX, NY - k // NX) + min(k % NX, NX - k % NX)

    far_first = sorted(range(1, PEERS), key=hops, reverse=True)
    far_depth = sorted(range(1, NZ), key=lambda k: min(k, NZ - k), reverse=True)

    barrier = pltpu.get_barrier_semaphore()
    peers = [(hops(k), {"sample": plane(k)}) for k in far_first]
    peers += [(min(k, NZ - k), depth(k)) for k in far_depth]
    for _, device in sorted(peers, key=lambda peer: -peer[0]):
        greet(barrier, device)
    greet(barrier, after, has_after)
    greet(barrier, before, has_before)

    @pl.when(jnp.logical_not(has_after))
    def _():
        g2[...] = jnp.zeros_like(g2)

    rows_f32[:, 0:8, :] = jnp.zeros((24, 8, 128), F32)
    rows_bf[:, :, :, 0:128] = jnp.zeros((3, 1, 16, 128), BF16)
    split_rows(x_halo[...], rows_f32, rows_bf, rows_sh, 0)
    acts = []
    for par in range(2):
        total = pre0[par]
        for b in range(3):
            total = total + dot(windows(rows_bf, par, 0, b), w_par[par, b])
        value, g = pointwise(total, cotangent_rows(cot_in, 0, par))
        acts.append(value)
        g0[par] = g
    turned = turn(perm, g0)

    quarter = lax.broadcasted_iota(jnp.int32, (COUT, 128), 1) // 32

    def full_tile(tap):
        return 9 * (tap // 4) + 2 * (tap % 4)

    def shared_tile(tap):
        return 20 if tap == 8 else 9 * (tap // 4) + 8

    def place(tile, value):
        for half in range(2):
            for block in range(6):
                at = HALF * half + 16 * block
                piece = value[at : at + 16]
                part[half, 6 * tile + block] = piece
                part_bf[half, 6 * tile + block] = piece.astype(BF16)

    for half in range(2):
        for block in range(6 * TILES, BLOCKS):
            part[half, block] = jnp.zeros((16, 128), F32)
            part_bf[half, block] = jnp.zeros((16, 128), BF16)
    shared = None
    for tap in range(9):
        a, b = tap // 3, tap % 3
        if a == 0:
            field = aligned_windows(rows_sh, 0, b)
        else:
            field = aligned_windows(rows_sh_in, a, b)
        total = part1[:, WIN * tap : WIN * tap + WIN] + dot(turned, field)
        place(full_tile(tap), total[:, 0:128])
        place(full_tile(tap) + 1, total[:, 128:256])
        rest = total[:, 256:384]
        if tap % 4 == 0:
            shared = rest
        else:
            shared = jnp.where(quarter == tap % 4, pltpu.roll(rest, 32 * (tap % 4), 1), shared)
        if tap % 4 == 3 or tap == 8:
            place(shared_tile(tap), shared)

    pl.semaphore_wait(barrier, neighbours + NZ - 1 + PEERS - 1)
    def units(c):
        return pl.ds(pl.multiple_of(UNITS * c, UNITS), UNITS)

    order = far_first + [0]
    core_copies = []
    for k in order:
        c = plane(k)
        copy = pltpu.make_async_remote_copy(
            src_ref=part_bf.at[1 - core, units(c)], dst_ref=core_in.at[units(c)],
            send_sem=core_send.at[k], recv_sem=core_recv.at[k],
            device_id=other, device_id_type=MESH,
        )
        copy.start()
        core_copies.append(copy)
    xy_copies = []
    for k, copy in zip(order, core_copies):
        copy.wait()
        c = plane(k)
        total = part[core, units(c)] + core_in[units(c)].astype(F32)
        if k == 0:
            own[...] = total
            break
        chunks[k - 1] = total.astype(BF16)
        copy = pltpu.make_async_remote_copy(
            src_ref=chunks.at[k - 1], dst_ref=chunk_in.at[k - 1],
            send_sem=xy_send.at[k - 1], recv_sem=xy_recv.at[k - 1],
            device_id={"sample": c}, device_id_type=MESH,
        )
        copy.start()
        xy_copies.append(copy)

    g_copy = pltpu.make_async_remote_copy(
        src_ref=g0, dst_ref=g2, send_sem=halo_send, recv_sem=halo_recv,
        device_id=before, device_id_type=MESH,
    )
    pl.when(has_before)(g_copy.start)
    side_by_side(acts[0], acts[1], act0)

    row = lax.broadcasted_iota(jnp.int32, (128, 256), 0)
    last_row = row % 16 == 15

    def shifted(value):
        up = pltpu.roll(value.astype(F32), 127, 0)
        return jnp.where(last_row, 0.0, up).astype(BF16)

    pl.when(has_before)(g_copy.wait_send)
    pl.when(has_after)(g_copy.wait_recv)
    g_rows = [[ref[par] for par in range(2)] for ref in (g0, g1, g2)]
    g_shift = [[shifted(g_rows[i][par]) for par in range(2)] for i in range(3)]

    def terms(par, first, row_par, a):
        def both(source):
            return jnp.concatenate([source[first][par], source[first + 1][par]], axis=0)

        if row_par == 0:
            return dot(both(g_rows), w_par[par, 3 * a + 1], NT)
        return dot(both(g_rows), w_par[par, 3 * a + 2], NT) + dot(
            both(g_shift), w_par[par, 3 * a], NT
        )

    for depth_par in range(2):
        for row_par in range(2):
            sums = []
            for par in range(2):
                if depth_par == 0:
                    sums.append(terms(par, 0, row_par, 1))
                else:
                    sums.append(terms(par, 0, row_par, 2) + terms(par, 1, row_par, 0))
            for i in range(2):
                for m in range(PAIRS):
                    at = 128 * i + 16 * m
                    value = sums[1][at : at + 16]
                    left = sums[0][at : at + 16, 128:]
                    if m < PAIRS - 1:
                        right = sums[0][at + 16 : at + 32, :128]
                    else:
                        right = jnp.zeros((16, 128), F32)
                    value = value + jnp.concatenate([left, right], axis=1)
                    for u in range(3):
                        piece = value[:, 128 * u : 128 * u + 128]
                        dx[2 * i + depth_par, 3 * m + u, pl.ds(row_par, 16, stride=2), :] = piece
    for d in range(4):
        for t in range(24):
            grad[d, :, 128 * t : 128 * t + 128] = dx[d, t].astype(BF16)

    total = own[...]
    for k, copy in zip(order, xy_copies):
        copy.wait()
        total = total + chunk_in[k - 1].astype(F32)
    summed[...] = total.reshape(16 * UNITS, 128)
    for k in range(NZ):
        for t in range(2):
            z_out[k, pl.ds(t, 8, stride=2), :] = summed[pl.ds(2 * k + t, 8, stride=16), :]

    z_copies = []
    for k in far_depth:
        copy = pltpu.make_async_remote_copy(
            src_ref=z_out.at[(z + k) % NZ], dst_ref=z_in.at[k - 1],
            send_sem=z_send.at[k - 1], recv_sem=z_recv.at[k - 1],
            device_id=depth(k), device_id_type=MESH,
        )
        copy.start()
        z_copies.append(copy)
    total = z_out[z]
    for k, copy in zip(far_depth, z_copies):
        copy.wait()
        total = total + z_in[k - 1]
    gathered[sample] = total * (1.0 / PEERS)

    ag_copies = []
    for k in far_first:
        copy = pltpu.make_async_remote_copy(
            src_ref=gathered.at[sample], dst_ref=gathered.at[sample],
            send_sem=ag_send.at[k - 1], recv_sem=ag_recv.at[k - 1],
            device_id={"sample": plane(k)}, device_id_type=MESH,
        )
        copy.start()
        ag_copies.append(copy)
    for copy in ag_copies:
        copy.wait()
    rows = gathered[...].reshape(16 * PEERS, 128)

    def tile_rows(tile):
        return rows[MINE * tile : MINE * tile + MINE]

    for tap in range(9):
        rest = tile_rows(shared_tile(tap))[:, 32 * (tap % 4) : 32 * (tap % 4) + 32]
        first = full_tile(tap)
        window = jnp.concatenate([tile_rows(first), tile_rows(first + 1), rest], axis=1)
        for e in range(3):
            wg[3 * tap + e] = window[:, 96 * e : 96 * e + 96]


def hand_over(act0, act1, grad, wg, act_hbm, grad_hbm, wg_hbm, sems):
    pairs = ((act0, act_hbm.at[0]), (act1, act_hbm.at[1]), (grad, grad_hbm), (wg, wg_hbm))
    copies = [
        pltpu.make_async_copy(src, dst, sems.at[n]) for n, (src, dst) in enumerate(pairs)
    ]
    for copy in copies:
        copy.start()
    for copy in copies:
        copy.wait()


def channel_order():
    table = np.zeros((COUT, 256), np.float32)
    for r in range(COUT):
        c, rest = divmod(r, HALF)
        block, inside = divmod(rest, 16)
        zz, t = divmod(inside, 2)
        table[r, (2 * zz + c) * MINE + 2 * block + t] = 1.0
    return jnp.asarray(table, BF16)


def per_device(slabs, weight, cotangent):
    any_space = pl.BlockSpec(memory_space=pl.ANY)
    on_chip = pl.BlockSpec(memory_space=pltpu.VMEM)
    in_hbm = pl.BlockSpec(memory_space=pltpu.HBM)
    dma = pltpu.SemaphoreType.DMA

    def held(array):
        return pltpu.with_memory_space_constraint(array, pltpu.VMEM)

    arguments = (
        slabs.reshape(4, 32, LANES),
        weight.reshape(9, 288, COUT),
        cotangent.reshape(2, 16, LANES),
        channel_order(),
    )
    *state, act1 = pl.pallas_call(
        first_kernel,
        out_shape=(
            pltpu.VMEM((32, LANES), BF16),
            pltpu.VMEM((2, 16, LANES), BF16),
            pltpu.VMEM((COUT, 256), BF16),
            pltpu.VMEM((2, 3, 5, 16, LANES + 128), BF16),
            pltpu.VMEM((2, 9, WIN, 256), BF16),
            pltpu.VMEM((2, 128, 256), F32),
            pltpu.VMEM((2, 128, 256), BF16),
            pltpu.VMEM((COUT, 9 * WIN), F32),
            pltpu.VMEM((16, LANES), BF16),
        ),
        in_specs=[in_hbm] * 4,
        out_specs=(on_chip,) * 9,
        scratch_shapes=[
            pltpu.VMEM((4, 32, LANES), BF16),
            pltpu.VMEM((9, 288, COUT), BF16),
            pltpu.VMEM((4, 24, 40, 128), F32),
            pltpu.VMEM((3, 5, 16, LANES + 128), BF16),
            dma((4,)), dma, dma,
        ],
        compiler_params=pltpu.CompilerParams(
            collective_id=0, has_side_effects=True, vmem_limit_bytes=16 << 20
        ),
        name="first_kernel",
    )(*(pltpu.with_memory_space_constraint(array, pltpu.HBM) for array in arguments))
    act0, grad, wg = pl.pallas_call(
        second_kernel,
        out_shape=(
            pltpu.VMEM((16, LANES), BF16),
            pltpu.VMEM((4, 32, LANES), BF16),
            pltpu.VMEM((27, MINE, 96), F32),
        ),
        in_specs=[on_chip] * 8,
        out_specs=(on_chip,) * 3,
        scratch_shapes=[
            pltpu.VMEM((24, 40, 128), F32),
            pltpu.VMEM((3, 1, 16, LANES + 128), BF16),
            pltpu.VMEM((2, 3, 1, 16, LANES + 128), BF16),
            pltpu.VMEM((2, 128, 256), BF16),
            pltpu.VMEM((2, 128, 256), BF16),
            pltpu.VMEM((2, BLOCKS, 16, 128), F32),
            pltpu.VMEM((2, BLOCKS, 16, 128), BF16),
            pltpu.VMEM((BLOCKS, 16, 128), BF16),
            pltpu.VMEM((UNITS, 16, 128), F32),
            pltpu.VMEM((PEERS - 1, UNITS, 16, 128), BF16),
            pltpu.VMEM((PEERS - 1, UNITS, 16, 128), BF16),
            pltpu.VMEM((128, 128), F32),
            pltpu.VMEM((NZ, 16, 128), F32),
            pltpu.VMEM((NZ - 1, 16, 128), F32),
            pltpu.VMEM((PEERS, 16, 128), F32),
            pltpu.VMEM((4, 24, 32, 128), F32),
            dma, dma, dma((PEERS,)), dma((PEERS,)),
            dma((PEERS - 1,)), dma((PEERS - 1,)), dma((NZ - 1,)), dma((NZ - 1,)),
            dma((PEERS - 1,)), dma((PEERS - 1,)),
        ],
        compiler_params=pltpu.CompilerParams(
            collective_id=1, has_side_effects=True, vmem_limit_bytes=32 << 20
        ),
        name="second_kernel",
    )(*(held(array) for array in state))
    activation, input_grad, gradient = pl.pallas_call(
        hand_over,
        out_shape=(
            jax.ShapeDtypeStruct((2, 16, LANES), BF16),
            jax.ShapeDtypeStruct((4, 32, LANES), BF16),
            jax.ShapeDtypeStruct((27, MINE, 96), F32),
        ),
        in_specs=[on_chip] * 4,
        out_specs=(any_space,) * 3,
        scratch_shapes=[dma((4,))],
        compiler_params=pltpu.CompilerParams(vmem_limit_bytes=4 << 20),
        name="hand_over",
    )(*(held(array) for array in (act0, act1, grad, wg)))
    return (
        activation.reshape(1, 2, 16, LANES),
        input_grad.reshape(1, 4, 32, LANES),
        jnp.swapaxes(gradient, 1, 2).reshape(3, 3, 3, 96, MINE),
    )


def solution(mesh):
    placed = (P("sample", "space", None, None), P(), P("sample", "space", None, None))
    return jax.shard_map(
        per_device,
        mesh=mesh,
        in_specs=placed,
        out_specs=(
            P("sample", "space", None, None),
            P("sample", "space", None, None),
            P(None, None, None, None, "space"),
        ),
        check_vma=False,
    )
```

```python
import functools

import jax
import jax.numpy as jnp
import numpy as np
from jax import lax
from jax.experimental import pallas as pl
from jax.experimental.pallas import tpu as pltpu
from jax.sharding import PartitionSpec as P

F32, BF16 = jnp.float32, jnp.bfloat16
MESH = pl.DeviceIdType.MESH

NY, NX, NZ = 4, 4, 8
PEERS = NY * NX
COUT = 192
LANES = 3072
PAIRS = 8
WIN = 384
HALF = COUT // 2
MINE = 12
TILES = 21
UNITS = 8
BLOCKS = UNITS * PEERS
NT = (((1,), (1,)), ((), ()))


def dot(a, b, dims=(((1,), (0,)), ((), ()))):
    return lax.dot_general(a, b, dims, preferred_element_type=F32)


def position():
    sample, space = lax.axis_index("sample"), lax.axis_index("space")
    after = {"space": (space + 1) % (2 * NZ)}
    before = {"space": (space + 2 * NZ - 1) % (2 * NZ)}
    return sample, space, after, before


def full_tile(tap):
    return 9 * (tap // 4) + 2 * (tap % 4)


def shared_tile(tap):
    return 20 if tap == 8 else 9 * (tap // 4) + 8


def greet(barrier, device, exists=None):
    def signal():
        pl.semaphore_signal(barrier, inc=1, device_id=device, device_id_type=MESH)

    if exists is None:
        signal()
    else:
        pl.when(exists)(signal)


def split_rows(values, rows_f32, rows_bf, rows_sh, d):
    for t in range(24):
        rows_f32[t, 8:40] = values[:, 128 * t : 128 * t + 128].astype(F32)
    lane = lax.broadcasted_iota(jnp.int32, (16, 128), 1)
    zero = jnp.zeros((16, 128), F32)
    for b in range(3):
        pieces = [rows_f32[t, pl.ds(7 + b, 16, stride=2), :] for t in range(24)]
        for t in range(24):
            rows_bf[b, d, :, 128 * t + 128 : 128 * t + 256] = pieces[t].astype(BF16)
        for n, left in enumerate((32, 96)):
            rolled = [pltpu.roll(piece, 128 - left, 1) for piece in pieces]
            for t in range(25):
                low = rolled[t - 1] if t > 0 else zero
                high = rolled[t] if t < 24 else zero
                piece = jnp.where(lane < 128 - left, low, high)
                rows_sh[n, b, d, :, 128 * t : 128 * t + 128] = piece.astype(BF16)


def windows(rows_bf, par, d, b):
    return jnp.concatenate(
        [
            rows_bf[b, d, :, 384 * m + 128 * par : 384 * m + 128 * par + WIN]
            for m in range(PAIRS)
        ],
        axis=0,
    )


def aligned_windows(rows_sh, d, b):
    return jnp.concatenate(
        [windows(rows_sh.at[par], par, d, b) for par in range(2)], axis=0
    )


def cotangent_rows(cot_in, i, par):
    cot = jnp.concatenate(
        [
            cot_in[i, :, 384 * m + 128 * par : 384 * m + 128 * par + 256]
            for m in range(PAIRS)
        ],
        axis=0,
    ).astype(F32)
    return pltpu.roll(cot, 192, 1) if par == 1 else cot


def pointwise(pre, cot):
    sigmoid_val = jax.nn.sigmoid(pre)
    g = cot * (sigmoid_val * (1.0 + pre * (1.0 - sigmoid_val)))
    return pre * sigmoid_val, g.astype(BF16)


def side_by_side(even, odd, out):
    low = lax.broadcasted_iota(jnp.int32, (128, 128), 1) < 64
    moved = pltpu.roll(odd, 64, 1)
    middle = jnp.where(low, even[:, 128:], moved[:, :128])
    dense = jnp.concatenate([even[:, :128], middle, moved[:, 128:]], axis=1).astype(BF16)
    for m in range(PAIRS):
        out[:, 384 * m : 384 * m + 384] = dense[16 * m : 16 * m + 16]


def turn(perm, g):
    return jnp.concatenate([dot(perm[...], g[par], NT).astype(BF16) for par in range(2)], axis=1)


def first_kernel(
    x_hbm, w_hbm, cot_hbm, perm_hbm,
    x_halo, cot_in, perm, rows_sh, w_par, pre0, g1, act1,
    x_in, w_in, rows_f32, rows_bf, load_sem, halo_send, halo_recv,
):
    _, space, after, before = position()
    has_before, has_after = space > 0, space < 2 * NZ - 1
    neighbours = 2 - jnp.where(has_before, 0, 1) - jnp.where(has_after, 0, 1)
    loads = [
        pltpu.make_async_copy(src, dst, load_sem.at[n])
        for n, (src, dst) in enumerate(
            ((x_hbm, x_in), (w_hbm, w_in), (cot_hbm, cot_in), (perm_hbm, perm))
        )
    ]
    for load in loads:
        load.start()
    barrier = pltpu.get_barrier_semaphore()
    @pl.when(jnp.logical_not(has_before))
    def _():
        x_halo[...] = jnp.zeros_like(x_halo)

    greet(barrier, after, has_after)
    greet(barrier, before, has_before)

    rows_f32[:, :, 0:8, :] = jnp.zeros((4, 24, 8, 128), F32)
    rows_bf[:, :, :, 0:128] = jnp.zeros((3, 5, 16, 128), BF16)
    loads[0].wait()
    x_copy = pltpu.make_async_remote_copy(
        src_ref=x_in.at[3], dst_ref=x_halo, send_sem=halo_send, recv_sem=halo_recv,
        device_id=after, device_id_type=MESH,
    )

    def send_plane():
        pl.semaphore_wait(barrier, neighbours)
        pl.when(has_after)(x_copy.start)

    core = space % 2
    pl.when(core == 1)(send_plane)
    for d in range(4):
        split_rows(x_in[d], rows_f32.at[d], rows_bf, rows_sh, d + 1)
    w_par[:, :, :, 128:] = jnp.zeros((2, 9, WIN, 128), BF16)
    w_par[0, :, 0:32, 0:128] = jnp.zeros((9, 32, 128), BF16)
    w_par[0, :, 320:, 0:128] = jnp.zeros((9, 64, 128), BF16)
    w_par[1, :, 0:96, 0:128] = jnp.zeros((9, 96, 128), BF16)
    loads[1].wait()
    w_par[0, :, 32:320, 0:COUT] = w_in[...]
    w_par[1, :, 96:384, 0:COUT] = w_in[...]

    pre1 = []
    for par in range(2):
        total0, total1 = None, None
        for tap in range(9):
            a, b = tap // 3, tap % 3
            high = windows(rows_bf, par, a + 2, b)
            if a == 0:
                term1 = dot(high, w_par[par, tap])
            else:
                both = dot(
                    jnp.concatenate([windows(rows_bf, par, a, b), high], axis=0), w_par[par, tap]
                )
                term1 = both[128:]
                total0 = both[:128] if total0 is None else total0 + both[:128]
            total1 = term1 if total1 is None else total1 + term1
        pre0[par] = total0
        pre1.append(total1)
    pl.when(core == 0)(send_plane)
    loads[2].wait()
    acts = []
    for par in range(2):
        value, g = pointwise(pre1[par], cotangent_rows(cot_in, 1, par))
        acts.append(value)
        g1[par] = g
    side_by_side(acts[0], acts[1], act1)
    loads[3].wait()
    pl.when(has_after)(x_copy.wait_send)
    pl.when(has_before)(x_copy.wait_recv)


def second_kernel(
    x_halo, cot_in, perm, rows_sh_in, w_par, pre0, g1,
    act0, grad, gathered,
    rows_f32, rows_bf, rows_sh, g0, g2, part, part_bf, core_in,
    own, chunks, chunk_in, summed, z_out, z_in, dx,
    halo_send, halo_recv, core_send, core_recv,
    xy_send, xy_recv, z_send, z_recv, ag_send, ag_recv,
):
    sample, space, after, before = position()
    has_before, has_after = space > 0, space < 2 * NZ - 1
    neighbours = 2 - jnp.where(has_before, 0, 1) - jnp.where(has_after, 0, 1)
    y, x = sample // NX, sample % NX
    z, core = space // 2, space % 2
    other = {"space": z * 2 + (1 - core)}

    def plane(k):
        return ((y + k // NX) % NY) * NX + (x + k % NX) % NX

    def depth(k):
        return {"space": ((z + k) % NZ) * 2 + core}

    def hops(k):
        return min(k // NX, NY - k // NX) + min(k % NX, NX - k % NX)

    far_first = sorted(range(1, PEERS), key=hops, reverse=True)
    far_depth = sorted(range(1, NZ), key=lambda k: min(k, NZ - k), reverse=True)

    barrier = pltpu.get_barrier_semaphore()
    peers = [(hops(k), {"sample": plane(k)}) for k in far_first]
    peers += [(min(k, NZ - k), depth(k)) for k in far_depth]
    for _, device in sorted(peers, key=lambda peer: -peer[0]):
        greet(barrier, device)
    greet(barrier, after, has_after)
    greet(barrier, before, has_before)

    @pl.when(jnp.logical_not(has_after))
    def _():
        g2[...] = jnp.zeros_like(g2)

    rows_f32[:, 0:8, :] = jnp.zeros((24, 8, 128), F32)
    rows_bf[:, :, :, 0:128] = jnp.zeros((3, 1, 16, 128), BF16)
    split_rows(x_halo[...], rows_f32, rows_bf, rows_sh, 0)
    acts = []
    for par in range(2):
        total = pre0[par]
        for b in range(3):
            total = total + dot(windows(rows_bf, par, 0, b), w_par[par, b])
        value, g = pointwise(total, cotangent_rows(cot_in, 0, par))
        acts.append(value)
        g0[par] = g
    turned = jnp.concatenate([turn(perm, g0), turn(perm, g1)], axis=1)

    quarter = lax.broadcasted_iota(jnp.int32, (COUT, 128), 1) // 32

    def place(tile, value):
        for half in range(2):
            for block in range(6):
                at = HALF * half + 16 * block
                piece = value[at : at + 16]
                part[half, 6 * tile + block] = piece
                part_bf[half, 6 * tile + block] = piece.astype(BF16)

    for half in range(2):
        for block in range(6 * TILES, BLOCKS):
            part[half, block] = jnp.zeros((16, 128), F32)
            part_bf[half, block] = jnp.zeros((16, 128), BF16)
    shared = None
    for tap in range(9):
        a, b = tap // 3, tap % 3
        low = aligned_windows(rows_sh, 0, b) if a == 0 else aligned_windows(rows_sh_in, a, b)
        total = dot(turned, jnp.concatenate([low, aligned_windows(rows_sh_in, a + 2, b)], axis=0))
        place(full_tile(tap), total[:, 0:128])
        place(full_tile(tap) + 1, total[:, 128:256])
        rest = total[:, 256:384]
        if tap % 4 == 0:
            shared = rest
        else:
            shared = jnp.where(quarter == tap % 4, pltpu.roll(rest, 32 * (tap % 4), 1), shared)
        if tap % 4 == 3 or tap == 8:
            place(shared_tile(tap), shared)

    pl.semaphore_wait(barrier, neighbours + NZ - 1 + PEERS - 1)
    def units(c):
        return pl.ds(pl.multiple_of(UNITS * c, UNITS), UNITS)

    order = far_first + [0]
    core_copies = []
    for k in order:
        c = plane(k)
        copy = pltpu.make_async_remote_copy(
            src_ref=part_bf.at[1 - core, units(c)], dst_ref=core_in.at[units(c)],
            send_sem=core_send.at[k], recv_sem=core_recv.at[k],
            device_id=other, device_id_type=MESH,
        )
        copy.start()
        core_copies.append(copy)
    xy_copies = []
    for k, copy in zip(order, core_copies):
        copy.wait()
        c = plane(k)
        total = part[core, units(c)] + core_in[units(c)].astype(F32)
        if k == 0:
            own[...] = total
            break
        chunks[k - 1] = total.astype(BF16)
        copy = pltpu.make_async_remote_copy(
            src_ref=chunks.at[k - 1], dst_ref=chunk_in.at[k - 1],
            send_sem=xy_send.at[k - 1], recv_sem=xy_recv.at[k - 1],
            device_id={"sample": c}, device_id_type=MESH,
        )
        copy.start()
        xy_copies.append(copy)

    g_copy = pltpu.make_async_remote_copy(
        src_ref=g0, dst_ref=g2, send_sem=halo_send, recv_sem=halo_recv,
        device_id=before, device_id_type=MESH,
    )
    pl.when(has_before)(g_copy.start)
    side_by_side(acts[0], acts[1], act0)

    row = lax.broadcasted_iota(jnp.int32, (128, 256), 0)
    last_row = row % 16 == 15

    def shifted(value):
        up = pltpu.roll(value.astype(F32), 127, 0)
        return jnp.where(last_row, 0.0, up).astype(BF16)

    pl.when(has_before)(g_copy.wait_send)
    pl.when(has_after)(g_copy.wait_recv)
    g_rows = [[ref[par] for par in range(2)] for ref in (g0, g1, g2)]
    g_shift = [[shifted(g_rows[i][par]) for par in range(2)] for i in range(3)]

    def terms(par, first, row_par, a):
        def both(source):
            return jnp.concatenate([source[first][par], source[first + 1][par]], axis=0)

        if row_par == 0:
            return dot(both(g_rows), w_par[par, 3 * a + 1], NT)
        return dot(both(g_rows), w_par[par, 3 * a + 2], NT) + dot(
            both(g_shift), w_par[par, 3 * a], NT
        )

    for depth_par in range(2):
        for row_par in range(2):
            sums = []
            for par in range(2):
                if depth_par == 0:
                    sums.append(terms(par, 0, row_par, 1))
                else:
                    sums.append(terms(par, 0, row_par, 2) + terms(par, 1, row_par, 0))
            for i in range(2):
                for m in range(PAIRS):
                    at = 128 * i + 16 * m
                    value = sums[1][at : at + 16]
                    left = sums[0][at : at + 16, 128:]
                    if m < PAIRS - 1:
                        right = sums[0][at + 16 : at + 32, :128]
                    else:
                        right = jnp.zeros((16, 128), F32)
                    value = value + jnp.concatenate([left, right], axis=1)
                    for u in range(3):
                        piece = value[:, 128 * u : 128 * u + 128]
                        dx[2 * i + depth_par, 3 * m + u, pl.ds(row_par, 16, stride=2), :] = piece
    for d in range(4):
        for t in range(24):
            grad[d, :, 128 * t : 128 * t + 128] = dx[d, t].astype(BF16)

    total = own[...]
    for k, copy in zip(order, xy_copies):
        copy.wait()
        total = total + chunk_in[k - 1].astype(F32)
    summed[...] = total.reshape(16 * UNITS, 128)
    for k in range(NZ):
        for t in range(2):
            z_out[k, pl.ds(t, 8, stride=2), :] = summed[pl.ds(2 * k + t, 8, stride=16), :]

    z_copies = []
    for k in far_depth:
        copy = pltpu.make_async_remote_copy(
            src_ref=z_out.at[(z + k) % NZ], dst_ref=z_in.at[k - 1],
            send_sem=z_send.at[k - 1], recv_sem=z_recv.at[k - 1],
            device_id=depth(k), device_id_type=MESH,
        )
        copy.start()
        z_copies.append(copy)
    total = z_out[z]
    for k, copy in zip(far_depth, z_copies):
        copy.wait()
        total = total + z_in[k - 1]
    mine = pl.ds(pl.multiple_of(16 * sample, 16), 16)
    gathered[mine] = total * (1.0 / PEERS)

    ag_copies = []
    for k in far_first:
        copy = pltpu.make_async_remote_copy(
            src_ref=gathered.at[mine], dst_ref=gathered.at[mine],
            send_sem=ag_send.at[k - 1], recv_sem=ag_recv.at[k - 1],
            device_id={"sample": plane(k)}, device_id_type=MESH,
        )
        copy.start()
        ag_copies.append(copy)
    for copy in ag_copies:
        copy.wait()


def hand_over(act0, act1, grad, gathered, act_hbm, grad_hbm, wg_hbm, wg, sems):
    pairs = ((act0, act_hbm.at[0]), (act1, act_hbm.at[1]), (grad, grad_hbm), (wg, wg_hbm))
    copies = [
        pltpu.make_async_copy(src, dst, sems.at[n]) for n, (src, dst) in enumerate(pairs)
    ]
    for copy in copies[:3]:
        copy.start()

    def tile_rows(tile):
        return gathered[MINE * tile : MINE * tile + MINE]

    for tap in range(9):
        rest = tile_rows(shared_tile(tap))[:, 32 * (tap % 4) : 32 * (tap % 4) + 32]
        first = full_tile(tap)
        window = jnp.concatenate([tile_rows(first), tile_rows(first + 1), rest], axis=1)
        for e in range(3):
            wg[3 * tap + e] = window[:, 96 * e : 96 * e + 96]
    copies[3].start()
    for copy in copies:
        copy.wait()


def channel_order():
    table = np.zeros((COUT, 256), np.float32)
    for r in range(COUT):
        c, rest = divmod(r, HALF)
        block, inside = divmod(rest, 16)
        zz, t = divmod(inside, 2)
        table[r, (2 * zz + c) * MINE + 2 * block + t] = 1.0
    return jnp.asarray(table, BF16)


def per_device(slabs, weight, cotangent):
    any_space = pl.BlockSpec(memory_space=pl.ANY)
    on_chip = pl.BlockSpec(memory_space=pltpu.VMEM)
    in_hbm = pl.BlockSpec(memory_space=pltpu.HBM)
    dma = pltpu.SemaphoreType.DMA

    def held(array):
        return pltpu.with_memory_space_constraint(array, pltpu.VMEM)

    arguments = (
        slabs.reshape(4, 32, LANES),
        weight.reshape(9, 288, COUT),
        cotangent.reshape(2, 16, LANES),
        channel_order(),
    )
    *state, act1 = pl.pallas_call(
        first_kernel,
        out_shape=(
            pltpu.VMEM((32, LANES), BF16),
            pltpu.VMEM((2, 16, LANES), BF16),
            pltpu.VMEM((COUT, 256), BF16),
            pltpu.VMEM((2, 3, 5, 16, LANES + 128), BF16),
            pltpu.VMEM((2, 9, WIN, 256), BF16),
            pltpu.VMEM((2, 128, 256), F32),
            pltpu.VMEM((2, 128, 256), BF16),
            pltpu.VMEM((16, LANES), BF16),
        ),
        in_specs=[in_hbm] * 4,
        out_specs=(on_chip,) * 8,
        scratch_shapes=[
            pltpu.VMEM((4, 32, LANES), BF16),
            pltpu.VMEM((9, 288, COUT), BF16),
            pltpu.VMEM((4, 24, 40, 128), F32),
            pltpu.VMEM((3, 5, 16, LANES + 128), BF16),
            dma((4,)), dma, dma,
        ],
        compiler_params=pltpu.CompilerParams(
            collective_id=0, has_side_effects=True, vmem_limit_bytes=16 << 20
        ),
        name="first_kernel",
    )(*(pltpu.with_memory_space_constraint(array, pltpu.HBM) for array in arguments))
    act0, grad, gathered = pl.pallas_call(
        second_kernel,
        out_shape=(
            pltpu.VMEM((16, LANES), BF16),
            pltpu.VMEM((4, 32, LANES), BF16),
            pltpu.VMEM((16 * PEERS, 128), F32),
        ),
        in_specs=[on_chip] * 7,
        out_specs=(on_chip,) * 3,
        scratch_shapes=[
            pltpu.VMEM((24, 40, 128), F32),
            pltpu.VMEM((3, 1, 16, LANES + 128), BF16),
            pltpu.VMEM((2, 3, 1, 16, LANES + 128), BF16),
            pltpu.VMEM((2, 128, 256), BF16),
            pltpu.VMEM((2, 128, 256), BF16),
            pltpu.VMEM((2, BLOCKS, 16, 128), F32),
            pltpu.VMEM((2, BLOCKS, 16, 128), BF16),
            pltpu.VMEM((BLOCKS, 16, 128), BF16),
            pltpu.VMEM((UNITS, 16, 128), F32),
            pltpu.VMEM((PEERS - 1, UNITS, 16, 128), BF16),
            pltpu.VMEM((PEERS - 1, UNITS, 16, 128), BF16),
            pltpu.VMEM((128, 128), F32),
            pltpu.VMEM((NZ, 16, 128), F32),
            pltpu.VMEM((NZ - 1, 16, 128), F32),
            pltpu.VMEM((4, 24, 32, 128), F32),
            dma, dma, dma((PEERS,)), dma((PEERS,)),
            dma((PEERS - 1,)), dma((PEERS - 1,)), dma((NZ - 1,)), dma((NZ - 1,)),
            dma((PEERS - 1,)), dma((PEERS - 1,)),
        ],
        compiler_params=pltpu.CompilerParams(
            collective_id=1, has_side_effects=True, vmem_limit_bytes=32 << 20
        ),
        name="second_kernel",
    )(*(held(array) for array in state))
    activation, input_grad, gradient = pl.pallas_call(
        hand_over,
        out_shape=(
            jax.ShapeDtypeStruct((2, 16, LANES), BF16),
            jax.ShapeDtypeStruct((4, 32, LANES), BF16),
            jax.ShapeDtypeStruct((27, MINE, 96), F32),
        ),
        in_specs=[on_chip] * 4,
        out_specs=(any_space,) * 3,
        scratch_shapes=[pltpu.VMEM((27, MINE, 96), F32), dma((4,))],
        compiler_params=pltpu.CompilerParams(vmem_limit_bytes=4 << 20),
        name="hand_over",
    )(*(held(array) for array in (act0, act1, grad, gathered)))
    return (
        activation.reshape(1, 2, 16, LANES),
        input_grad.reshape(1, 4, 32, LANES),
        jnp.swapaxes(gradient, 1, 2).reshape(3, 3, 3, 96, MINE),
    )


def solution(mesh):
    placed = (P("sample", "space", None, None), P(), P("sample", "space", None, None))
    return jax.shard_map(
        per_device,
        mesh=mesh,
        in_specs=placed,
        out_specs=(
            P("sample", "space", None, None),
            P("sample", "space", None, None),
            P(None, None, None, None, "space"),
        ),
        check_vma=False,
    )
```

```python
import functools

import jax
import jax.numpy as jnp
import numpy as np
from jax import lax
from jax.experimental import pallas as pl
from jax.experimental.pallas import tpu as pltpu
from jax.sharding import PartitionSpec as P

F32, BF16 = jnp.float32, jnp.bfloat16
MESH = pl.DeviceIdType.MESH

NY, NX, NZ = 4, 4, 8
PEERS = NY * NX
COUT = 192
LANES = 3072
PAIRS = 8
WIN = 384
HALF = COUT // 2
MINE = 12
TILES = 21
UNITS = 8
BLOCKS = UNITS * PEERS
NT = (((1,), (1,)), ((), ()))


def dot(a, b, dims=(((1,), (0,)), ((), ()))):
    return lax.dot_general(a, b, dims, preferred_element_type=F32)


def position():
    sample, space = lax.axis_index("sample"), lax.axis_index("space")
    after = {"space": (space + 1) % (2 * NZ)}
    before = {"space": (space + 2 * NZ - 1) % (2 * NZ)}
    return sample, space, after, before


def full_tile(tap):
    return 9 * (tap // 4) + 2 * (tap % 4)


def shared_tile(tap):
    return 20 if tap == 8 else 9 * (tap // 4) + 8


def greet(barrier, device, exists=None):
    def signal():
        pl.semaphore_signal(barrier, inc=1, device_id=device, device_id_type=MESH)

    if exists is None:
        signal()
    else:
        pl.when(exists)(signal)


def split_rows(values, rows_f32, rows_bf, rows_sh, d):
    for t in range(24):
        rows_f32[t, 8:40] = values[:, 128 * t : 128 * t + 128].astype(F32)
    lane = lax.broadcasted_iota(jnp.int32, (16, 128), 1)
    zero = jnp.zeros((16, 128), F32)
    for b in range(3):
        pieces = [rows_f32[t, pl.ds(7 + b, 16, stride=2), :] for t in range(24)]
        for t in range(24):
            rows_bf[b, d, :, 128 * t + 128 : 128 * t + 256] = pieces[t].astype(BF16)
        for n, left in enumerate((32, 96)):
            rolled = [pltpu.roll(piece, 128 - left, 1) for piece in pieces]
            for t in range(25):
                low = rolled[t - 1] if t > 0 else zero
                high = rolled[t] if t < 24 else zero
                piece = jnp.where(lane < 128 - left, low, high)
                rows_sh[n, b, d, :, 128 * t : 128 * t + 128] = piece.astype(BF16)


def windows(rows_bf, par, d, b):
    return jnp.concatenate(
        [
            rows_bf[b, d, :, 384 * m + 128 * par : 384 * m + 128 * par + WIN]
            for m in range(PAIRS)
        ],
        axis=0,
    )


def aligned_windows(rows_sh, d, b):
    return jnp.concatenate(
        [windows(rows_sh.at[par], par, d, b) for par in range(2)], axis=0
    )


def cotangent_rows(cot_in, i, par):
    cot = jnp.concatenate(
        [
            cot_in[i, :, 384 * m + 128 * par : 384 * m + 128 * par + 256]
            for m in range(PAIRS)
        ],
        axis=0,
    ).astype(F32)
    return pltpu.roll(cot, 192, 1) if par == 1 else cot


def pointwise(pre, cot):
    sigmoid_val = jax.nn.sigmoid(pre)
    g = cot * (sigmoid_val * (1.0 + pre * (1.0 - sigmoid_val)))
    return pre * sigmoid_val, g.astype(BF16)


def side_by_side(even, odd, out):
    low = lax.broadcasted_iota(jnp.int32, (128, 128), 1) < 64
    moved = pltpu.roll(odd, 64, 1)
    middle = jnp.where(low, even[:, 128:], moved[:, :128])
    dense = jnp.concatenate([even[:, :128], middle, moved[:, 128:]], axis=1).astype(BF16)
    for m in range(PAIRS):
        out[:, 384 * m : 384 * m + 384] = dense[16 * m : 16 * m + 16]


def turn(perm, g):
    return jnp.concatenate([dot(perm[...], g[par], NT).astype(BF16) for par in range(2)], axis=1)


def first_kernel(
    x_hbm, w_hbm, cot_hbm, perm_hbm,
    x_halo, cot_in, perm, rows_sh, w_par, pre0, g1, act1,
    x_in, w_in, rows_f32, rows_bf, load_sem, halo_send, halo_recv,
):
    _, space, after, before = position()
    has_before, has_after = space > 0, space < 2 * NZ - 1
    neighbours = 2 - jnp.where(has_before, 0, 1) - jnp.where(has_after, 0, 1)
    loads = [
        pltpu.make_async_copy(src, dst, load_sem.at[n])
        for n, (src, dst) in enumerate(
            ((x_hbm, x_in), (w_hbm, w_in), (cot_hbm, cot_in), (perm_hbm, perm))
        )
    ]
    for load in loads:
        load.start()
    barrier = pltpu.get_barrier_semaphore()
    @pl.when(jnp.logical_not(has_before))
    def _():
        x_halo[...] = jnp.zeros_like(x_halo)

    greet(barrier, after, has_after)
    greet(barrier, before, has_before)

    rows_f32[:, :, 0:8, :] = jnp.zeros((4, 24, 8, 128), F32)
    rows_bf[:, :, :, 0:128] = jnp.zeros((3, 5, 16, 128), BF16)
    loads[0].wait()
    x_copy = pltpu.make_async_remote_copy(
        src_ref=x_in.at[3], dst_ref=x_halo, send_sem=halo_send, recv_sem=halo_recv,
        device_id=after, device_id_type=MESH,
    )

    def send_plane():
        pl.semaphore_wait(barrier, neighbours)
        pl.when(has_after)(x_copy.start)

    core = space % 2
    pl.when(core == 1)(send_plane)
    for d in range(4):
        split_rows(x_in[d], rows_f32.at[d], rows_bf, rows_sh, d + 1)
    w_par[:, :, :, 128:] = jnp.zeros((2, 9, WIN, 128), BF16)
    w_par[0, :, 0:32, 0:128] = jnp.zeros((9, 32, 128), BF16)
    w_par[0, :, 320:, 0:128] = jnp.zeros((9, 64, 128), BF16)
    w_par[1, :, 0:96, 0:128] = jnp.zeros((9, 96, 128), BF16)
    loads[1].wait()
    w_par[0, :, 32:320, 0:COUT] = w_in[...]
    w_par[1, :, 96:384, 0:COUT] = w_in[...]

    pre1 = []
    for par in range(2):
        total0, total1 = None, None
        for tap in range(9):
            a, b = tap // 3, tap % 3
            high = windows(rows_bf, par, a + 2, b)
            if a == 0:
                term1 = dot(high, w_par[par, tap])
            else:
                both = dot(
                    jnp.concatenate([windows(rows_bf, par, a, b), high], axis=0), w_par[par, tap]
                )
                term1 = both[128:]
                total0 = both[:128] if total0 is None else total0 + both[:128]
            total1 = term1 if total1 is None else total1 + term1
        pre0[par] = total0
        pre1.append(total1)
    pl.when(core == 0)(send_plane)
    loads[2].wait()
    acts = []
    for par in range(2):
        value, g = pointwise(pre1[par], cotangent_rows(cot_in, 1, par))
        acts.append(value)
        g1[par] = g
    side_by_side(acts[0], acts[1], act1)
    loads[3].wait()
    pl.when(has_after)(x_copy.wait_send)
    pl.when(has_before)(x_copy.wait_recv)


def second_kernel(
    x_halo, cot_in, perm, rows_sh_in, w_par, pre0, g1,
    act0, grad, gathered,
    rows_f32, rows_bf, rows_sh, g0, g2, part, part_bf, core_in,
    own, chunks, chunk_in, summed, z_out, z_in, dx,
    halo_send, halo_recv, core_send, core_recv,
    xy_send, xy_recv, z_send, z_recv, ag_send, ag_recv,
):
    sample, space, after, before = position()
    has_before, has_after = space > 0, space < 2 * NZ - 1
    neighbours = 2 - jnp.where(has_before, 0, 1) - jnp.where(has_after, 0, 1)
    y, x = sample // NX, sample % NX
    z, core = space // 2, space % 2
    other = {"space": z * 2 + (1 - core)}

    def plane(k):
        return ((y + k // NX) % NY) * NX + (x + k % NX) % NX

    def depth(k):
        return {"space": ((z + k) % NZ) * 2 + core}

    def hops(k):
        return min(k // NX, NY - k // NX) + min(k % NX, NX - k % NX)

    far_first = sorted(range(1, PEERS), key=hops, reverse=True)
    far_depth = sorted(range(1, NZ), key=lambda k: min(k, NZ - k), reverse=True)

    barrier = pltpu.get_barrier_semaphore()
    peers = [(hops(k), {"sample": plane(k)}) for k in far_first]
    peers += [(min(k, NZ - k), depth(k)) for k in far_depth]
    for _, device in sorted(peers, key=lambda peer: -peer[0]):
        greet(barrier, device)
    greet(barrier, after, has_after)
    greet(barrier, before, has_before)

    @pl.when(jnp.logical_not(has_after))
    def _():
        g2[...] = jnp.zeros_like(g2)

    rows_f32[:, 0:8, :] = jnp.zeros((24, 8, 128), F32)
    rows_bf[:, :, :, 0:128] = jnp.zeros((3, 1, 16, 128), BF16)
    split_rows(x_halo[...], rows_f32, rows_bf, rows_sh, 0)
    acts = []
    for par in range(2):
        total = pre0[par]
        for b in range(3):
            total = total + dot(windows(rows_bf, par, 0, b), w_par[par, b])
        value, g = pointwise(total, cotangent_rows(cot_in, 0, par))
        acts.append(value)
        g0[par] = g
    turned = jnp.concatenate([turn(perm, g0), turn(perm, g1)], axis=1)

    quarter = lax.broadcasted_iota(jnp.int32, (COUT, 128), 1) // 32

    def place(tile, value):
        for half in range(2):
            for block in range(6):
                at = HALF * half + 16 * block
                piece = value[at : at + 16]
                part[half, 6 * tile + block] = piece
                part_bf[half, 6 * tile + block] = piece.astype(BF16)

    for half in range(2):
        for block in range(6 * TILES, BLOCKS):
            part[half, block] = jnp.zeros((16, 128), F32)
            part_bf[half, block] = jnp.zeros((16, 128), BF16)
    shared = None
    for tap in range(9):
        a, b = tap // 3, tap % 3
        low = aligned_windows(rows_sh, 0, b) if a == 0 else aligned_windows(rows_sh_in, a, b)
        total = dot(turned, jnp.concatenate([low, aligned_windows(rows_sh_in, a + 2, b)], axis=0))
        place(full_tile(tap), total[:, 0:128])
        place(full_tile(tap) + 1, total[:, 128:256])
        rest = total[:, 256:384]
        if tap % 4 == 0:
            shared = rest
        else:
            shared = jnp.where(quarter == tap % 4, pltpu.roll(rest, 32 * (tap % 4), 1), shared)
        if tap % 4 == 3 or tap == 8:
            place(shared_tile(tap), shared)

    pl.semaphore_wait(barrier, neighbours + NZ - 1 + PEERS - 1)
    def units(c):
        return pl.ds(pl.multiple_of(UNITS * c, UNITS), UNITS)

    order = far_first + [0]
    core_copies = []
    for k in order:
        c = plane(k)
        copy = pltpu.make_async_remote_copy(
            src_ref=part_bf.at[1 - core, units(c)], dst_ref=core_in.at[units(c)],
            send_sem=core_send.at[k], recv_sem=core_recv.at[k],
            device_id=other, device_id_type=MESH,
        )
        copy.start()
        core_copies.append(copy)
    xy_copies = []
    for k, copy in zip(order, core_copies):
        copy.wait()
        c = plane(k)
        total = part[core, units(c)] + core_in[units(c)].astype(F32)
        if k == 0:
            own[...] = total
            break
        chunks[k - 1] = total.astype(BF16)
        copy = pltpu.make_async_remote_copy(
            src_ref=chunks.at[k - 1], dst_ref=chunk_in.at[k - 1],
            send_sem=xy_send.at[k - 1], recv_sem=xy_recv.at[k - 1],
            device_id={"sample": c}, device_id_type=MESH,
        )
        copy.start()
        xy_copies.append(copy)

    g_copy = pltpu.make_async_remote_copy(
        src_ref=g0, dst_ref=g2, send_sem=halo_send, recv_sem=halo_recv,
        device_id=before, device_id_type=MESH,
    )
    pl.when(has_before)(g_copy.start)
    side_by_side(acts[0], acts[1], act0)

    row = lax.broadcasted_iota(jnp.int32, (128, 256), 0)
    last_row = row % 16 == 15

    def shifted(value):
        up = pltpu.roll(value.astype(F32), 127, 0)
        return jnp.where(last_row, 0.0, up).astype(BF16)

    pl.when(has_before)(g_copy.wait_send)
    pl.when(has_after)(g_copy.wait_recv)
    g_rows = [[ref[par] for par in range(2)] for ref in (g0, g1, g2)]
    g_shift = [[shifted(g_rows[i][par]) for par in range(2)] for i in range(3)]

    def terms(par, first, row_par, a):
        def both(source):
            return jnp.concatenate([source[first][par], source[first + 1][par]], axis=0)

        if row_par == 0:
            return dot(both(g_rows), w_par[par, 3 * a + 1], NT)
        return dot(both(g_rows), w_par[par, 3 * a + 2], NT) + dot(
            both(g_shift), w_par[par, 3 * a], NT
        )

    for depth_par in range(2):
        for row_par in range(2):
            sums = []
            for par in range(2):
                if depth_par == 0:
                    sums.append(terms(par, 0, row_par, 1))
                else:
                    sums.append(terms(par, 0, row_par, 2) + terms(par, 1, row_par, 0))
            for i in range(2):
                for m in range(PAIRS):
                    at = 128 * i + 16 * m
                    value = sums[1][at : at + 16]
                    left = sums[0][at : at + 16, 128:]
                    if m < PAIRS - 1:
                        right = sums[0][at + 16 : at + 32, :128]
                    else:
                        right = jnp.zeros((16, 128), F32)
                    value = value + jnp.concatenate([left, right], axis=1)
                    for u in range(3):
                        piece = value[:, 128 * u : 128 * u + 128]
                        dx[2 * i + depth_par, 3 * m + u, pl.ds(row_par, 16, stride=2), :] = piece
    for d in range(4):
        for t in range(24):
            grad[d, :, 128 * t : 128 * t + 128] = dx[d, t, 0:32].astype(BF16)

    total = own[...]
    for k, copy in zip(order, xy_copies):
        copy.wait()
        total = total + chunk_in[k - 1].astype(F32)
    summed[0:128] = total.reshape(16 * UNITS, 128)
    for k in range(NZ):
        for t in range(2):
            z_out[k, pl.ds(t, 8, stride=2), :] = summed[pl.ds(2 * k + t, 8, stride=16), :]

    z_copies = []
    for k in far_depth:
        copy = pltpu.make_async_remote_copy(
            src_ref=z_out.at[(z + k) % NZ, 0:16], dst_ref=z_in.at[k - 1],
            send_sem=z_send.at[k - 1], recv_sem=z_recv.at[k - 1],
            device_id=depth(k), device_id_type=MESH,
        )
        copy.start()
        z_copies.append(copy)
    total = z_out[z, 0:16]
    for k, copy in zip(far_depth, z_copies):
        copy.wait()
        total = total + z_in[k - 1]
    mine = pl.ds(pl.multiple_of(16 * sample, 16), 16)
    gathered[mine] = total * (1.0 / PEERS)

    ag_copies = []
    for k in far_first:
        copy = pltpu.make_async_remote_copy(
            src_ref=gathered.at[mine], dst_ref=gathered.at[mine],
            send_sem=ag_send.at[k - 1], recv_sem=ag_recv.at[k - 1],
            device_id={"sample": plane(k)}, device_id_type=MESH,
        )
        copy.start()
        ag_copies.append(copy)
    for copy in ag_copies:
        copy.wait()


def hand_over(act0, act1, grad, gathered, act_hbm, grad_hbm, wg_hbm, wg, sems):
    pairs = ((act0, act_hbm.at[0]), (act1, act_hbm.at[1]), (grad, grad_hbm), (wg, wg_hbm))
    copies = [
        pltpu.make_async_copy(src, dst, sems.at[n]) for n, (src, dst) in enumerate(pairs)
    ]
    for copy in copies[:3]:
        copy.start()

    def tile_rows(tile):
        return gathered[MINE * tile : MINE * tile + MINE]

    for tap in range(9):
        rest = tile_rows(shared_tile(tap))[:, 32 * (tap % 4) : 32 * (tap % 4) + 32]
        first = full_tile(tap)
        window = jnp.concatenate([tile_rows(first), tile_rows(first + 1), rest], axis=1)
        for e in range(3):
            wg[3 * tap + e] = window[:, 96 * e : 96 * e + 96]
    copies[3].start()
    for copy in copies:
        copy.wait()


def channel_order():
    table = np.zeros((COUT, 256), np.float32)
    for r in range(COUT):
        c, rest = divmod(r, HALF)
        block, inside = divmod(rest, 16)
        zz, t = divmod(inside, 2)
        table[r, (2 * zz + c) * MINE + 2 * block + t] = 1.0
    return jnp.asarray(table, BF16)


def per_device(slabs, weight, cotangent):
    any_space = pl.BlockSpec(memory_space=pl.ANY)
    on_chip = pl.BlockSpec(memory_space=pltpu.VMEM)
    in_hbm = pl.BlockSpec(memory_space=pltpu.HBM)
    dma = pltpu.SemaphoreType.DMA

    def held(array):
        return pltpu.with_memory_space_constraint(array, pltpu.VMEM)

    arguments = (
        slabs.reshape(4, 32, LANES),
        weight.reshape(9, 288, COUT),
        cotangent.reshape(2, 16, LANES),
        channel_order(),
    )
    *state, act1 = pl.pallas_call(
        first_kernel,
        out_shape=(
            pltpu.VMEM((32, LANES), BF16),
            pltpu.VMEM((2, 16, LANES), BF16),
            pltpu.VMEM((COUT, 256), BF16),
            pltpu.VMEM((2, 3, 5, 16, LANES + 128), BF16),
            pltpu.VMEM((2, 9, WIN, 256), BF16),
            pltpu.VMEM((2, 128, 256), F32),
            pltpu.VMEM((2, 128, 256), BF16),
            pltpu.VMEM((16, LANES), BF16),
        ),
        in_specs=[in_hbm] * 4,
        out_specs=(on_chip,) * 8,
        scratch_shapes=[
            pltpu.VMEM((4, 32, LANES), BF16),
            pltpu.VMEM((9, 288, COUT), BF16),
            pltpu.VMEM((4, 24, 48, 128), F32),
            pltpu.VMEM((3, 5, 16, LANES + 128), BF16),
            dma((4,)), dma, dma,
        ],
        compiler_params=pltpu.CompilerParams(
            collective_id=0, has_side_effects=True, vmem_limit_bytes=16 << 20
        ),
        name="first_kernel",
    )(*(pltpu.with_memory_space_constraint(array, pltpu.HBM) for array in arguments))
    act0, grad, gathered = pl.pallas_call(
        second_kernel,
        out_shape=(
            pltpu.VMEM((16, LANES), BF16),
            pltpu.VMEM((4, 32, LANES), BF16),
            pltpu.VMEM((16 * PEERS, 128), F32),
        ),
        in_specs=[on_chip] * 7,
        out_specs=(on_chip,) * 3,
        scratch_shapes=[
            pltpu.VMEM((24, 48, 128), F32),
            pltpu.VMEM((3, 1, 16, LANES + 128), BF16),
            pltpu.VMEM((2, 3, 1, 16, LANES + 128), BF16),
            pltpu.VMEM((2, 128, 256), BF16),
            pltpu.VMEM((2, 128, 256), BF16),
            pltpu.VMEM((2, BLOCKS, 16, 128), F32),
            pltpu.VMEM((2, BLOCKS, 16, 128), BF16),
            pltpu.VMEM((BLOCKS, 16, 128), BF16),
            pltpu.VMEM((UNITS, 16, 128), F32),
            pltpu.VMEM((PEERS - 1, UNITS, 16, 128), BF16),
            pltpu.VMEM((PEERS - 1, UNITS, 16, 128), BF16),
            pltpu.VMEM((144, 128), F32),
            pltpu.VMEM((NZ, 24, 128), F32),
            pltpu.VMEM((NZ - 1, 16, 128), F32),
            pltpu.VMEM((4, 24, 40, 128), F32),
            dma, dma, dma((PEERS,)), dma((PEERS,)),
            dma((PEERS - 1,)), dma((PEERS - 1,)), dma((NZ - 1,)), dma((NZ - 1,)),
            dma((PEERS - 1,)), dma((PEERS - 1,)),
        ],
        compiler_params=pltpu.CompilerParams(
            collective_id=1, has_side_effects=True, vmem_limit_bytes=32 << 20
        ),
        name="second_kernel",
    )(*(held(array) for array in state))
    activation, input_grad, gradient = pl.pallas_call(
        hand_over,
        out_shape=(
            jax.ShapeDtypeStruct((2, 16, LANES), BF16),
            jax.ShapeDtypeStruct((4, 32, LANES), BF16),
            jax.ShapeDtypeStruct((27, MINE, 96), F32),
        ),
        in_specs=[on_chip] * 4,
        out_specs=(any_space,) * 3,
        scratch_shapes=[pltpu.VMEM((27, MINE, 96), F32), dma((4,))],
        compiler_params=pltpu.CompilerParams(vmem_limit_bytes=4 << 20),
        name="hand_over",
    )(*(held(array) for array in (act0, act1, grad, gathered)))
    return (
        activation.reshape(1, 2, 16, LANES),
        input_grad.reshape(1, 4, 32, LANES),
        jnp.swapaxes(gradient, 1, 2).reshape(3, 3, 3, 96, MINE),
    )


def solution(mesh):
    placed = (P("sample", "space", None, None), P(), P("sample", "space", None, None))
    return jax.shard_map(
        per_device,
        mesh=mesh,
        in_specs=placed,
        out_specs=(
            P("sample", "space", None, None),
            P("sample", "space", None, None),
            P(None, None, None, None, "space"),
        ),
        check_vma=False,
    )
```

```python
import functools

import jax
import jax.numpy as jnp
import numpy as np
from jax import lax
from jax.experimental import pallas as pl
from jax.experimental.pallas import tpu as pltpu
from jax.sharding import PartitionSpec as P

F32, BF16 = jnp.float32, jnp.bfloat16
MESH = pl.DeviceIdType.MESH

NY, NX, NZ = 4, 4, 8
PEERS = NY * NX
COUT = 192
LANES = 3072
PAIRS = 8
WIN = 384
HALF = COUT // 2
MINE = 12
TILES = 21
UNITS = 8
BLOCKS = UNITS * PEERS
NT = (((1,), (1,)), ((), ()))


def dot(a, b, dims=(((1,), (0,)), ((), ()))):
    return lax.dot_general(a, b, dims, preferred_element_type=F32)


def position():
    sample, space = lax.axis_index("sample"), lax.axis_index("space")
    after = {"space": (space + 1) % (2 * NZ)}
    before = {"space": (space + 2 * NZ - 1) % (2 * NZ)}
    return sample, space, after, before


def full_tile(tap):
    return 9 * (tap // 4) + 2 * (tap % 4)


def shared_tile(tap):
    return 20 if tap == 8 else 9 * (tap // 4) + 8


def greet(barrier, device, exists=None):
    def signal():
        pl.semaphore_signal(barrier, inc=1, device_id=device, device_id_type=MESH)

    if exists is None:
        signal()
    else:
        pl.when(exists)(signal)


def split_rows(values, rows_f32, rows_bf, rows_sh, d):
    for t in range(24):
        rows_f32[t, 8:40] = values[:, 128 * t : 128 * t + 128].astype(F32)
    lane = lax.broadcasted_iota(jnp.int32, (16, 128), 1)
    zero = jnp.zeros((16, 128), F32)
    for b in range(3):
        pieces = [rows_f32[t, pl.ds(7 + b, 16, stride=2), :] for t in range(24)]
        for t in range(24):
            rows_bf[b, d, :, 128 * t + 128 : 128 * t + 256] = pieces[t].astype(BF16)
        for n, left in enumerate((32, 96)):
            rolled = [pltpu.roll(piece, 128 - left, 1) for piece in pieces]
            for t in range(25):
                low = rolled[t - 1] if t > 0 else zero
                high = rolled[t] if t < 24 else zero
                piece = jnp.where(lane < 128 - left, low, high)
                rows_sh[n, b, d, :, 128 * t : 128 * t + 128] = piece.astype(BF16)


def windows(rows_bf, par, d, b):
    return jnp.concatenate(
        [
            rows_bf[b, d, :, 384 * m + 128 * par : 384 * m + 128 * par + WIN]
            for m in range(PAIRS)
        ],
        axis=0,
    )


def aligned_windows(rows_sh, d, b):
    return jnp.concatenate(
        [windows(rows_sh.at[par], par, d, b) for par in range(2)], axis=0
    )


def cotangent_rows(cot_in, i, par):
    cot = jnp.concatenate(
        [
            cot_in[i, :, 384 * m + 128 * par : 384 * m + 128 * par + 256]
            for m in range(PAIRS)
        ],
        axis=0,
    ).astype(F32)
    return pltpu.roll(cot, 192, 1) if par == 1 else cot


def pointwise(pre, cot):
    sigmoid_val = jax.nn.sigmoid(pre)
    g = cot * (sigmoid_val * (1.0 + pre * (1.0 - sigmoid_val)))
    return pre * sigmoid_val, g.astype(BF16)


def side_by_side(even, odd, out):
    low = lax.broadcasted_iota(jnp.int32, (128, 128), 1) < 64
    moved = pltpu.roll(odd, 64, 1)
    middle = jnp.where(low, even[:, 128:], moved[:, :128])
    dense = jnp.concatenate([even[:, :128], middle, moved[:, 128:]], axis=1).astype(BF16)
    for m in range(PAIRS):
        out[:, 384 * m : 384 * m + 384] = dense[16 * m : 16 * m + 16]


def turn(perm, g):
    return jnp.concatenate([dot(perm[...], g[par], NT).astype(BF16) for par in range(2)], axis=1)


def first_kernel(
    x_hbm, w_hbm, cot_hbm, perm_hbm,
    x_halo, cot_in, perm, rows_sh, w_par, pre0, g1, act1,
    x_in, w_in, rows_f32, rows_bf, load_sem, halo_send, halo_recv,
):
    _, space, after, before = position()
    has_before, has_after = space > 0, space < 2 * NZ - 1
    neighbours = 2 - jnp.where(has_before, 0, 1) - jnp.where(has_after, 0, 1)
    loads = [
        pltpu.make_async_copy(src, dst, load_sem.at[n])
        for n, (src, dst) in enumerate(
            ((x_hbm, x_in), (w_hbm, w_in), (cot_hbm, cot_in), (perm_hbm, perm))
        )
    ]
    for load in loads:
        load.start()
    barrier = pltpu.get_barrier_semaphore()
    @pl.when(jnp.logical_not(has_before))
    def _():
        x_halo[...] = jnp.zeros_like(x_halo)

    greet(barrier, after, has_after)
    greet(barrier, before, has_before)

    rows_f32[:, :, 0:8, :] = jnp.zeros((4, 24, 8, 128), F32)
    rows_bf[:, :, :, 0:128] = jnp.zeros((3, 5, 16, 128), BF16)
    loads[0].wait()
    x_copy = pltpu.make_async_remote_copy(
        src_ref=x_in.at[3], dst_ref=x_halo, send_sem=halo_send, recv_sem=halo_recv,
        device_id=after, device_id_type=MESH,
    )

    def send_plane():
        pl.semaphore_wait(barrier, neighbours)
        pl.when(has_after)(x_copy.start)

    core = space % 2
    pl.when(core == 1)(send_plane)
    for d in range(4):
        split_rows(x_in[d], rows_f32.at[d], rows_bf, rows_sh, d + 1)
    w_par[:, :, :, 128:] = jnp.zeros((2, 9, WIN, 128), BF16)
    w_par[0, :, 0:32, 0:128] = jnp.zeros((9, 32, 128), BF16)
    w_par[0, :, 320:, 0:128] = jnp.zeros((9, 64, 128), BF16)
    w_par[1, :, 0:96, 0:128] = jnp.zeros((9, 96, 128), BF16)
    loads[1].wait()
    w_par[0, :, 32:320, 0:COUT] = w_in[...]
    w_par[1, :, 96:384, 0:COUT] = w_in[...]

    pre1 = []
    for par in range(2):
        total0, total1 = None, None
        for tap in range(9):
            a, b = tap // 3, tap % 3
            high = windows(rows_bf, par, a + 2, b)
            if a == 0:
                term1 = dot(high, w_par[par, tap])
            else:
                both = dot(
                    jnp.concatenate([windows(rows_bf, par, a, b), high], axis=0), w_par[par, tap]
                )
                term1 = both[128:]
                total0 = both[:128] if total0 is None else total0 + both[:128]
            total1 = term1 if total1 is None else total1 + term1
        pre0[par] = total0
        pre1.append(total1)
    pl.when(core == 0)(send_plane)
    loads[2].wait()
    acts = []
    for par in range(2):
        value, g = pointwise(pre1[par], cotangent_rows(cot_in, 1, par))
        acts.append(value)
        g1[par] = g
    side_by_side(acts[0], acts[1], act1)
    loads[3].wait()
    pl.when(has_after)(x_copy.wait_send)
    pl.when(has_before)(x_copy.wait_recv)


def second_kernel(
    x_halo, cot_in, perm, rows_sh_in, w_par, pre0, g1,
    act0, grad, gathered,
    rows_f32, rows_bf, rows_sh, g0, g2, part, part_bf, core_in,
    own, chunks, chunk_in, summed, z_out, z_in, dx,
    halo_send, halo_recv, core_send, core_recv,
    xy_send, xy_recv, z_send, z_recv, ag_send, ag_recv,
):
    sample, space, after, before = position()
    has_before, has_after = space > 0, space < 2 * NZ - 1
    neighbours = 2 - jnp.where(has_before, 0, 1) - jnp.where(has_after, 0, 1)
    y, x = sample // NX, sample % NX
    z, core = space // 2, space % 2
    other = {"space": z * 2 + (1 - core)}

    def plane(k):
        return ((y + k // NX) % NY) * NX + (x + k % NX) % NX

    def mirrored(k, side):
        dy, dx_ = k // NX, k % NX
        dy, dx_ = dy + side * (NY - 2 * dy), dx_ + side * (NX - 2 * dx_)
        return ((y + dy) % NY) * NX + (x + dx_) % NX

    def depth(k):
        return {"space": ((z + k) % NZ) * 2 + core}

    def hops(k):
        return min(k // NX, NY - k // NX) + min(k % NX, NX - k % NX)

    far_first = sorted(range(1, PEERS), key=hops, reverse=True)
    far_depth = sorted(range(1, NZ), key=lambda k: min(k, NZ - k), reverse=True)

    barrier = pltpu.get_barrier_semaphore()
    peers = [(hops(k), {"sample": plane(k)}) for k in far_first]
    peers += [(min(k, NZ - k), depth(k)) for k in far_depth]
    for _, device in sorted(peers, key=lambda peer: -peer[0]):
        greet(barrier, device)
    greet(barrier, after, has_after)
    greet(barrier, before, has_before)

    @pl.when(jnp.logical_not(has_after))
    def _():
        g2[...] = jnp.zeros_like(g2)

    rows_f32[:, 0:8, :] = jnp.zeros((24, 8, 128), F32)
    rows_bf[:, :, :, 0:128] = jnp.zeros((3, 1, 16, 128), BF16)
    split_rows(x_halo[...], rows_f32, rows_bf, rows_sh, 0)
    acts = []
    for par in range(2):
        total = pre0[par]
        for b in range(3):
            total = total + dot(windows(rows_bf, par, 0, b), w_par[par, b])
        value, g = pointwise(total, cotangent_rows(cot_in, 0, par))
        acts.append(value)
        g0[par] = g
    turned = jnp.concatenate([turn(perm, g0), turn(perm, g1)], axis=1)

    quarter = lax.broadcasted_iota(jnp.int32, (COUT, 128), 1) // 32

    def place(tile, value):
        for half in range(2):
            for block in range(6):
                at = HALF * half + 16 * block
                piece = value[at : at + 16]
                part[half, 6 * tile + block] = piece
                part_bf[half, 6 * tile + block] = piece.astype(BF16)

    for half in range(2):
        for block in range(6 * TILES, BLOCKS):
            part[half, block] = jnp.zeros((16, 128), F32)
            part_bf[half, block] = jnp.zeros((16, 128), BF16)
    shared = None
    for tap in range(9):
        a, b = tap // 3, tap % 3
        low = aligned_windows(rows_sh, 0, b) if a == 0 else aligned_windows(rows_sh_in, a, b)
        total = dot(turned, jnp.concatenate([low, aligned_windows(rows_sh_in, a + 2, b)], axis=0))
        place(full_tile(tap), total[:, 0:128])
        place(full_tile(tap) + 1, total[:, 128:256])
        rest = total[:, 256:384]
        if tap % 4 == 0:
            shared = rest
        else:
            shared = jnp.where(quarter == tap % 4, pltpu.roll(rest, 32 * (tap % 4), 1), shared)
        if tap % 4 == 3 or tap == 8:
            place(shared_tile(tap), shared)

    pl.semaphore_wait(barrier, neighbours + NZ - 1 + PEERS - 1)
    def units(c):
        return pl.ds(pl.multiple_of(UNITS * c, UNITS), UNITS)

    order = far_first + [0]
    core_copies = []
    for k in order:
        c = mirrored(k, 1 - core)
        copy = pltpu.make_async_remote_copy(
            src_ref=part_bf.at[1 - core, units(c)], dst_ref=core_in.at[units(c)],
            send_sem=core_send.at[k], recv_sem=core_recv.at[k],
            device_id=other, device_id_type=MESH,
        )
        copy.start()
        core_copies.append(copy)
    xy_copies = []
    for k, copy in zip(order, core_copies):
        copy.wait()
        c = mirrored(k, core)
        total = part[core, units(c)] + core_in[units(c)].astype(F32)
        if k == 0:
            own[...] = total
            break
        chunks[k - 1] = total.astype(BF16)
        copy = pltpu.make_async_remote_copy(
            src_ref=chunks.at[k - 1], dst_ref=chunk_in.at[k - 1],
            send_sem=xy_send.at[k - 1], recv_sem=xy_recv.at[k - 1],
            device_id={"sample": c}, device_id_type=MESH,
        )
        copy.start()
        xy_copies.append(copy)

    g_copy = pltpu.make_async_remote_copy(
        src_ref=g0, dst_ref=g2, send_sem=halo_send, recv_sem=halo_recv,
        device_id=before, device_id_type=MESH,
    )
    pl.when(has_before)(g_copy.start)
    side_by_side(acts[0], acts[1], act0)

    row = lax.broadcasted_iota(jnp.int32, (128, 256), 0)
    last_row = row % 16 == 15

    def shifted(value):
        up = pltpu.roll(value.astype(F32), 127, 0)
        return jnp.where(last_row, 0.0, up).astype(BF16)

    pl.when(has_before)(g_copy.wait_send)
    pl.when(has_after)(g_copy.wait_recv)
    g_rows = [[ref[par] for par in range(2)] for ref in (g0, g1, g2)]
    g_shift = [[shifted(g_rows[i][par]) for par in range(2)] for i in range(3)]

    def terms(par, first, row_par, a):
        def both(source):
            return jnp.concatenate([source[first][par], source[first + 1][par]], axis=0)

        if row_par == 0:
            return dot(both(g_rows), w_par[par, 3 * a + 1], NT)
        return dot(both(g_rows), w_par[par, 3 * a + 2], NT) + dot(
            both(g_shift), w_par[par, 3 * a], NT
        )

    for depth_par in range(2):
        for row_par in range(2):
            sums = []
            for par in range(2):
                if depth_par == 0:
                    sums.append(terms(par, 0, row_par, 1))
                else:
                    sums.append(terms(par, 0, row_par, 2) + terms(par, 1, row_par, 0))
            for i in range(2):
                for m in range(PAIRS):
                    at = 128 * i + 16 * m
                    value = sums[1][at : at + 16]
                    left = sums[0][at : at + 16, 128:]
                    if m < PAIRS - 1:
                        right = sums[0][at + 16 : at + 32, :128]
                    else:
                        right = jnp.zeros((16, 128), F32)
                    value = value + jnp.concatenate([left, right], axis=1)
                    for u in range(3):
                        piece = value[:, 128 * u : 128 * u + 128]
                        dx[2 * i + depth_par, 3 * m + u, pl.ds(row_par, 16, stride=2), :] = piece
    for d in range(4):
        for t in range(24):
            grad[d, :, 128 * t : 128 * t + 128] = dx[d, t, 0:32].astype(BF16)

    total = own[...]
    for k, copy in zip(order, xy_copies):
        copy.wait()
        total = total + chunk_in[k - 1].astype(F32)
    summed[0:128] = total.reshape(16 * UNITS, 128)
    for k in range(NZ):
        for t in range(2):
            z_out[k, pl.ds(t, 8, stride=2), :] = summed[pl.ds(2 * k + t, 8, stride=16), :]

    z_copies = []
    for k in far_depth:
        copy = pltpu.make_async_remote_copy(
            src_ref=z_out.at[(z + k) % NZ, 0:16], dst_ref=z_in.at[k - 1],
            send_sem=z_send.at[k - 1], recv_sem=z_recv.at[k - 1],
            device_id=depth(k), device_id_type=MESH,
        )
        copy.start()
        z_copies.append(copy)
    total = z_out[z, 0:16]
    for k, copy in zip(far_depth, z_copies):
        copy.wait()
        total = total + z_in[k - 1]
    mine = pl.ds(pl.multiple_of(16 * sample, 16), 16)
    gathered[mine] = total * (1.0 / PEERS)

    ag_copies = []
    for k in far_first:
        copy = pltpu.make_async_remote_copy(
            src_ref=gathered.at[mine], dst_ref=gathered.at[mine],
            send_sem=ag_send.at[k - 1], recv_sem=ag_recv.at[k - 1],
            device_id={"sample": plane(k)}, device_id_type=MESH,
        )
        copy.start()
        ag_copies.append(copy)
    for copy in ag_copies:
        copy.wait()


def hand_over(act0, act1, grad, gathered, act_hbm, grad_hbm, wg_hbm, wg, sems):
    pairs = ((act0, act_hbm.at[0]), (act1, act_hbm.at[1]), (grad, grad_hbm), (wg, wg_hbm))
    copies = [
        pltpu.make_async_copy(src, dst, sems.at[n]) for n, (src, dst) in enumerate(pairs)
    ]
    for copy in copies[:3]:
        copy.start()

    def tile_rows(tile):
        return gathered[MINE * tile : MINE * tile + MINE]

    for tap in range(9):
        rest = tile_rows(shared_tile(tap))[:, 32 * (tap % 4) : 32 * (tap % 4) + 32]
        first = full_tile(tap)
        window = jnp.concatenate([tile_rows(first), tile_rows(first + 1), rest], axis=1)
        for e in range(3):
            wg[3 * tap + e] = window[:, 96 * e : 96 * e + 96]
    copies[3].start()
    for copy in copies:
        copy.wait()


def channel_order():
    table = np.zeros((COUT, 256), np.float32)
    for r in range(COUT):
        c, rest = divmod(r, HALF)
        block, inside = divmod(rest, 16)
        zz, t = divmod(inside, 2)
        table[r, (2 * zz + c) * MINE + 2 * block + t] = 1.0
    return jnp.asarray(table, BF16)


def per_device(slabs, weight, cotangent):
    any_space = pl.BlockSpec(memory_space=pl.ANY)
    on_chip = pl.BlockSpec(memory_space=pltpu.VMEM)
    in_hbm = pl.BlockSpec(memory_space=pltpu.HBM)
    dma = pltpu.SemaphoreType.DMA

    def held(array):
        return pltpu.with_memory_space_constraint(array, pltpu.VMEM)

    arguments = (
        slabs.reshape(4, 32, LANES),
        weight.reshape(9, 288, COUT),
        cotangent.reshape(2, 16, LANES),
        channel_order(),
    )
    *state, act1 = pl.pallas_call(
        first_kernel,
        out_shape=(
            pltpu.VMEM((32, LANES), BF16),
            pltpu.VMEM((2, 16, LANES), BF16),
            pltpu.VMEM((COUT, 256), BF16),
            pltpu.VMEM((2, 3, 5, 16, LANES + 128), BF16),
            pltpu.VMEM((2, 9, WIN, 256), BF16),
            pltpu.VMEM((2, 128, 256), F32),
            pltpu.VMEM((2, 128, 256), BF16),
            pltpu.VMEM((16, LANES), BF16),
        ),
        in_specs=[in_hbm] * 4,
        out_specs=(on_chip,) * 8,
        scratch_shapes=[
            pltpu.VMEM((4, 32, LANES), BF16),
            pltpu.VMEM((9, 288, COUT), BF16),
            pltpu.VMEM((4, 24, 48, 128), F32),
            pltpu.VMEM((3, 5, 16, LANES + 128), BF16),
            dma((4,)), dma, dma,
        ],
        compiler_params=pltpu.CompilerParams(
            collective_id=0, has_side_effects=True, vmem_limit_bytes=16 << 20
        ),
        name="first_kernel",
    )(*(pltpu.with_memory_space_constraint(array, pltpu.HBM) for array in arguments))
    act0, grad, gathered = pl.pallas_call(
        second_kernel,
        out_shape=(
            pltpu.VMEM((16, LANES), BF16),
            pltpu.VMEM((4, 32, LANES), BF16),
            pltpu.VMEM((16 * PEERS, 128), F32),
        ),
        in_specs=[on_chip] * 7,
        out_specs=(on_chip,) * 3,
        scratch_shapes=[
            pltpu.VMEM((24, 48, 128), F32),
            pltpu.VMEM((3, 1, 16, LANES + 128), BF16),
            pltpu.VMEM((2, 3, 1, 16, LANES + 128), BF16),
            pltpu.VMEM((2, 128, 256), BF16),
            pltpu.VMEM((2, 128, 256), BF16),
            pltpu.VMEM((2, BLOCKS, 16, 128), F32),
            pltpu.VMEM((2, BLOCKS, 16, 128), BF16),
            pltpu.VMEM((BLOCKS, 16, 128), BF16),
            pltpu.VMEM((UNITS, 16, 128), F32),
            pltpu.VMEM((PEERS - 1, UNITS, 16, 128), BF16),
            pltpu.VMEM((PEERS - 1, UNITS, 16, 128), BF16),
            pltpu.VMEM((144, 128), F32),
            pltpu.VMEM((NZ, 24, 128), F32),
            pltpu.VMEM((NZ - 1, 16, 128), F32),
            pltpu.VMEM((4, 24, 40, 128), F32),
            dma, dma, dma((PEERS,)), dma((PEERS,)),
            dma((PEERS - 1,)), dma((PEERS - 1,)), dma((NZ - 1,)), dma((NZ - 1,)),
            dma((PEERS - 1,)), dma((PEERS - 1,)),
        ],
        compiler_params=pltpu.CompilerParams(
            collective_id=1, has_side_effects=True, vmem_limit_bytes=32 << 20
        ),
        name="second_kernel",
    )(*(held(array) for array in state))
    activation, input_grad, gradient = pl.pallas_call(
        hand_over,
        out_shape=(
            jax.ShapeDtypeStruct((2, 16, LANES), BF16),
            jax.ShapeDtypeStruct((4, 32, LANES), BF16),
            jax.ShapeDtypeStruct((27, MINE, 96), F32),
        ),
        in_specs=[on_chip] * 4,
        out_specs=(any_space,) * 3,
        scratch_shapes=[pltpu.VMEM((27, MINE, 96), F32), dma((4,))],
        compiler_params=pltpu.CompilerParams(vmem_limit_bytes=4 << 20),
        name="hand_over",
    )(*(held(array) for array in (act0, act1, grad, gathered)))
    return (
        activation.reshape(1, 2, 16, LANES),
        input_grad.reshape(1, 4, 32, LANES),
        jnp.swapaxes(gradient, 1, 2).reshape(3, 3, 3, 96, MINE),
    )


def solution(mesh):
    placed = (P("sample", "space", None, None), P(), P("sample", "space", None, None))
    return jax.shard_map(
        per_device,
        mesh=mesh,
        in_specs=placed,
        out_specs=(
            P("sample", "space", None, None),
            P("sample", "space", None, None),
            P(None, None, None, None, "space"),
        ),
        check_vma=False,
    )
```

```python
import functools

import jax
import jax.numpy as jnp
import numpy as np
from jax import lax
from jax.experimental import pallas as pl
from jax.experimental.pallas import tpu as pltpu
from jax.sharding import PartitionSpec as P

F32, BF16 = jnp.float32, jnp.bfloat16
MESH = pl.DeviceIdType.MESH

NY, NX, NZ = 4, 4, 8
PEERS = NY * NX
COUT = 192
LANES = 3072
PAIRS = 8
WIN = 384
HALF = COUT // 2
MINE = 12
TILES = 21
UNITS = 8
BLOCKS = UNITS * PEERS
NT = (((1,), (1,)), ((), ()))


def dot(a, b, dims=(((1,), (0,)), ((), ()))):
    return lax.dot_general(a, b, dims, preferred_element_type=F32)


def position():
    sample, space = lax.axis_index("sample"), lax.axis_index("space")
    after = {"space": (space + 1) % (2 * NZ)}
    before = {"space": (space + 2 * NZ - 1) % (2 * NZ)}
    return sample, space, after, before


def full_tile(tap):
    return 9 * (tap // 4) + 2 * (tap % 4)


def shared_tile(tap):
    return 20 if tap == 8 else 9 * (tap // 4) + 8


def greet(barrier, device, exists=None):
    def signal():
        pl.semaphore_signal(barrier, inc=1, device_id=device, device_id_type=MESH)

    if exists is None:
        signal()
    else:
        pl.when(exists)(signal)


def split_rows(values, rows_f32, rows_bf, rows_sh, d):
    for t in range(24):
        rows_f32[t, 8:40] = values[:, 128 * t : 128 * t + 128].astype(F32)
    lane = lax.broadcasted_iota(jnp.int32, (16, 128), 1)
    zero = jnp.zeros((16, 128), F32)
    for b in range(3):
        pieces = [rows_f32[t, pl.ds(7 + b, 16, stride=2), :] for t in range(24)]
        for t in range(24):
            rows_bf[b, d, :, 128 * t + 128 : 128 * t + 256] = pieces[t].astype(BF16)
        for n, left in enumerate((32, 96)):
            rolled = [pltpu.roll(piece, 128 - left, 1) for piece in pieces]
            for t in range(25):
                low = rolled[t - 1] if t > 0 else zero
                high = rolled[t] if t < 24 else zero
                piece = jnp.where(lane < 128 - left, low, high)
                rows_sh[n, b, d, :, 128 * t : 128 * t + 128] = piece.astype(BF16)


def windows(rows_bf, par, d, b):
    return jnp.concatenate(
        [
            rows_bf[b, d, :, 384 * m + 128 * par : 384 * m + 128 * par + WIN]
            for m in range(PAIRS)
        ],
        axis=0,
    )


def aligned_windows(rows_sh, d, b):
    return jnp.concatenate(
        [windows(rows_sh.at[par], par, d, b) for par in range(2)], axis=0
    )


def cotangent_rows(cot_in, i, par):
    cot = jnp.concatenate(
        [
            cot_in[i, :, 384 * m + 128 * par : 384 * m + 128 * par + 256]
            for m in range(PAIRS)
        ],
        axis=0,
    ).astype(F32)
    return pltpu.roll(cot, 192, 1) if par == 1 else cot


def pointwise(pre, cot):
    sigmoid_val = jax.nn.sigmoid(pre)
    g = cot * (sigmoid_val * (1.0 + pre * (1.0 - sigmoid_val)))
    return pre * sigmoid_val, g.astype(BF16)


def side_by_side(even, odd, out):
    low = lax.broadcasted_iota(jnp.int32, (128, 128), 1) < 64
    moved = pltpu.roll(odd, 64, 1)
    middle = jnp.where(low, even[:, 128:], moved[:, :128])
    dense = jnp.concatenate([even[:, :128], middle, moved[:, 128:]], axis=1).astype(BF16)
    for m in range(PAIRS):
        out[:, 384 * m : 384 * m + 384] = dense[16 * m : 16 * m + 16]


def turn(perm, g):
    return jnp.concatenate([dot(perm[...], g[par], NT).astype(BF16) for par in range(2)], axis=1)


def first_kernel(
    x_hbm, w_hbm, cot_hbm, perm_hbm,
    x_halo, cot_in, perm, rows_sh, w_par, pre0, g1, act1,
    x_in, w_in, rows_f32, rows_bf, load_sem, halo_send, halo_recv,
):
    _, space, after, before = position()
    has_before, has_after = space > 0, space < 2 * NZ - 1
    neighbours = 2 - jnp.where(has_before, 0, 1) - jnp.where(has_after, 0, 1)
    loads = [
        pltpu.make_async_copy(src, dst, load_sem.at[n])
        for n, (src, dst) in enumerate(
            ((x_hbm, x_in), (w_hbm, w_in), (cot_hbm, cot_in), (perm_hbm, perm))
        )
    ]
    for load in loads:
        load.start()
    barrier = pltpu.get_barrier_semaphore()
    @pl.when(jnp.logical_not(has_before))
    def _():
        x_halo[...] = jnp.zeros_like(x_halo)

    greet(barrier, after, has_after)
    greet(barrier, before, has_before)

    rows_f32[:, :, 0:8, :] = jnp.zeros((4, 24, 8, 128), F32)
    rows_bf[:, :, :, 0:128] = jnp.zeros((3, 5, 16, 128), BF16)
    loads[0].wait()
    x_copy = pltpu.make_async_remote_copy(
        src_ref=x_in.at[3], dst_ref=x_halo, send_sem=halo_send, recv_sem=halo_recv,
        device_id=after, device_id_type=MESH,
    )

    def send_plane():
        pl.semaphore_wait(barrier, neighbours)
        pl.when(has_after)(x_copy.start)

    core = space % 2
    pl.when(core == 1)(send_plane)
    for d in range(4):
        split_rows(x_in[d], rows_f32.at[d], rows_bf, rows_sh, d + 1)
    w_par[:, :, :, 128:] = jnp.zeros((2, 9, WIN, 128), BF16)
    w_par[0, :, 0:32, 0:128] = jnp.zeros((9, 32, 128), BF16)
    w_par[0, :, 320:, 0:128] = jnp.zeros((9, 64, 128), BF16)
    w_par[1, :, 0:96, 0:128] = jnp.zeros((9, 96, 128), BF16)
    loads[1].wait()
    w_par[0, :, 32:320, 0:COUT] = w_in[...]
    w_par[1, :, 96:384, 0:COUT] = w_in[...]

    pre1 = []
    for par in range(2):
        total0, total1 = None, None
        for tap in range(9):
            a, b = tap // 3, tap % 3
            high = windows(rows_bf, par, a + 2, b)
            if a == 0:
                term1 = dot(high, w_par[par, tap])
            else:
                both = dot(
                    jnp.concatenate([windows(rows_bf, par, a, b), high], axis=0), w_par[par, tap]
                )
                term1 = both[128:]
                total0 = both[:128] if total0 is None else total0 + both[:128]
            total1 = term1 if total1 is None else total1 + term1
        pre0[par] = total0
        pre1.append(total1)
    pl.when(core == 0)(send_plane)
    loads[2].wait()
    acts = []
    for par in range(2):
        value, g = pointwise(pre1[par], cotangent_rows(cot_in, 1, par))
        acts.append(value)
        g1[par] = g
    side_by_side(acts[0], acts[1], act1)
    loads[3].wait()
    pl.when(has_after)(x_copy.wait_send)
    pl.when(has_before)(x_copy.wait_recv)


def second_kernel(
    x_halo, cot_in, perm, rows_sh_in, w_par, pre0, g1,
    act0, grad, gathered,
    rows_f32, rows_bf, rows_sh, g0, g2, part, part_bf, core_in,
    own, chunks, chunk_in, summed, z_out, z_in, dx,
    halo_send, halo_recv, core_send, core_recv,
    xy_send, xy_recv, z_send, z_recv, ag_send, ag_recv,
):
    sample, space, after, before = position()
    has_before, has_after = space > 0, space < 2 * NZ - 1
    neighbours = 2 - jnp.where(has_before, 0, 1) - jnp.where(has_after, 0, 1)
    y, x = sample // NX, sample % NX
    z, core = space // 2, space % 2
    other = {"space": z * 2 + (1 - core)}

    def plane(k):
        return ((y + k // NX) % NY) * NX + (x + k % NX) % NX

    def mirrored(k, side):
        dy, dx_ = k // NX, k % NX
        dy, dx_ = dy + side * (NY - 2 * dy), dx_ + side * (NX - 2 * dx_)
        return ((y + dy) % NY) * NX + (x + dx_) % NX

    def depth(k):
        return {"space": ((z + k) % NZ) * 2 + core}

    def hops(k):
        return min(k // NX, NY - k // NX) + min(k % NX, NX - k % NX)

    far_first = sorted(range(1, PEERS), key=hops, reverse=True)
    far_depth = sorted(range(1, NZ), key=lambda k: min(k, NZ - k), reverse=True)

    barrier = pltpu.get_barrier_semaphore()
    peers = [(hops(k), {"sample": plane(k)}) for k in far_first]
    peers += [(min(k, NZ - k), depth(k)) for k in far_depth]
    for _, device in sorted(peers, key=lambda peer: -peer[0]):
        greet(barrier, device)
    greet(barrier, after, has_after)
    greet(barrier, before, has_before)

    @pl.when(jnp.logical_not(has_after))
    def _():
        g2[...] = jnp.zeros_like(g2)

    rows_f32[:, 0:8, :] = jnp.zeros((24, 8, 128), F32)
    rows_bf[:, :, :, 0:128] = jnp.zeros((3, 1, 16, 128), BF16)
    split_rows(x_halo[...], rows_f32, rows_bf, rows_sh, 0)
    acts = []
    for par in range(2):
        total = pre0[par]
        for b in range(3):
            total = total + dot(windows(rows_bf, par, 0, b), w_par[par, b])
        value, g = pointwise(total, cotangent_rows(cot_in, 0, par))
        acts.append(value)
        g0[par] = g
    turned = jnp.concatenate([turn(perm, g0), turn(perm, g1)], axis=1)

    quarter = lax.broadcasted_iota(jnp.int32, (COUT, 128), 1) // 32

    def place(tile, value):
        for half in range(2):
            for block in range(6):
                at = HALF * half + 16 * block
                piece = value[at : at + 16]
                part[half, 6 * tile + block] = piece
                part_bf[half, 6 * tile + block] = piece.astype(BF16)

    for half in range(2):
        for block in range(6 * TILES, BLOCKS):
            part[half, block] = jnp.zeros((16, 128), F32)
            part_bf[half, block] = jnp.zeros((16, 128), BF16)
    shared = None
    for tap in range(9):
        a, b = tap // 3, tap % 3
        low = aligned_windows(rows_sh, 0, b) if a == 0 else aligned_windows(rows_sh_in, a, b)
        total = dot(turned, jnp.concatenate([low, aligned_windows(rows_sh_in, a + 2, b)], axis=0))
        place(full_tile(tap), total[:, 0:128])
        place(full_tile(tap) + 1, total[:, 128:256])
        rest = total[:, 256:384]
        if tap % 4 == 0:
            shared = rest
        else:
            shared = jnp.where(quarter == tap % 4, pltpu.roll(rest, 32 * (tap % 4), 1), shared)
        if tap % 4 == 3 or tap == 8:
            place(shared_tile(tap), shared)

    pl.semaphore_wait(barrier, neighbours + NZ - 1 + PEERS - 1)
    def units(c):
        return pl.ds(pl.multiple_of(UNITS * c, UNITS), UNITS)

    order = far_first + [0]
    core_copies = []
    for k in order:
        c = mirrored(k, 1 - core)
        copy = pltpu.make_async_remote_copy(
            src_ref=part_bf.at[1 - core, units(c)], dst_ref=core_in.at[units(c)],
            send_sem=core_send.at[k], recv_sem=core_recv.at[k],
            device_id=other, device_id_type=MESH,
        )
        copy.start()
        core_copies.append(copy)
    xy_copies = []
    for k, copy in zip(order, core_copies):
        copy.wait()
        c = mirrored(k, core)
        total = part[core, units(c)] + core_in[units(c)].astype(F32)
        if k == 0:
            own[...] = total
            break
        chunks[k - 1] = total.astype(BF16)
        copy = pltpu.make_async_remote_copy(
            src_ref=chunks.at[k - 1], dst_ref=chunk_in.at[k - 1],
            send_sem=xy_send.at[k - 1], recv_sem=xy_recv.at[k - 1],
            device_id={"sample": c}, device_id_type=MESH,
        )
        copy.start()
        xy_copies.append(copy)

    g_copy = pltpu.make_async_remote_copy(
        src_ref=g0, dst_ref=g2, send_sem=halo_send, recv_sem=halo_recv,
        device_id=before, device_id_type=MESH,
    )
    pl.when(has_before)(g_copy.start)
    side_by_side(acts[0], acts[1], act0)

    row = lax.broadcasted_iota(jnp.int32, (128, 256), 0)
    last_row = row % 16 == 15

    def shifted(value):
        up = pltpu.roll(value.astype(F32), 127, 0)
        return jnp.where(last_row, 0.0, up).astype(BF16)

    pl.when(has_before)(g_copy.wait_send)
    pl.when(has_after)(g_copy.wait_recv)
    g_rows = [[ref[par] for par in range(2)] for ref in (g0, g1, g2)]
    g_shift = [[shifted(g_rows[i][par]) for par in range(2)] for i in range(3)]

    def terms(par, first, row_par, a):
        def both(source):
            return jnp.concatenate([source[first][par], source[first + 1][par]], axis=0)

        if row_par == 0:
            return dot(both(g_rows), w_par[par, 3 * a + 1], NT)
        return dot(both(g_rows), w_par[par, 3 * a + 2], NT) + dot(
            both(g_shift), w_par[par, 3 * a], NT
        )

    for depth_par in range(2):
        for row_par in range(2):
            sums = []
            for par in range(2):
                if depth_par == 0:
                    sums.append(terms(par, 0, row_par, 1))
                else:
                    sums.append(terms(par, 0, row_par, 2) + terms(par, 1, row_par, 0))
            for i in range(2):
                for m in range(PAIRS):
                    at = 128 * i + 16 * m
                    value = sums[1][at : at + 16]
                    left = sums[0][at : at + 16, 128:]
                    if m < PAIRS - 1:
                        right = sums[0][at + 16 : at + 32, :128]
                    else:
                        right = jnp.zeros((16, 128), F32)
                    value = value + jnp.concatenate([left, right], axis=1)
                    for u in range(3):
                        piece = value[:, 128 * u : 128 * u + 128]
                        dx[2 * i + depth_par, 3 * m + u, pl.ds(row_par, 16, stride=2), :] = piece
    for d in range(4):
        for t in range(24):
            grad[d, :, 128 * t : 128 * t + 128] = dx[d, t, 0:32].astype(BF16)

    total = own[...]
    for k, copy in zip(order, xy_copies):
        copy.wait()
        total = total + chunk_in[k - 1].astype(F32)
    summed[0:128] = total.reshape(16 * UNITS, 128)
    for k in range(NZ):
        for t in range(2):
            z_out[k, pl.ds(t, 8, stride=2), :] = summed[pl.ds(2 * k + t, 8, stride=16), :]

    z_copies = []
    for k in far_depth:
        copy = pltpu.make_async_remote_copy(
            src_ref=z_out.at[(z + k) % NZ, 0:16], dst_ref=z_in.at[k - 1],
            send_sem=z_send.at[k - 1], recv_sem=z_recv.at[k - 1],
            device_id=depth(k), device_id_type=MESH,
        )
        copy.start()
        z_copies.append(copy)
    total = z_out[z, 0:16]
    for k, copy in zip(far_depth, z_copies):
        copy.wait()
        total = total + z_in[k - 1]
    mine = pl.ds(pl.multiple_of(16 * sample, 16), 16)
    gathered[mine] = total * (1.0 / PEERS)

    ag_copies = []
    for k in far_first:
        copy = pltpu.make_async_remote_copy(
            src_ref=gathered.at[mine], dst_ref=gathered.at[mine],
            send_sem=ag_send.at[k - 1], recv_sem=ag_recv.at[k - 1],
            device_id={"sample": mirrored(k, core)}, device_id_type=MESH,
        )
        copy.start()
        ag_copies.append(copy)
    for copy in ag_copies:
        copy.wait()


def hand_over(act0, act1, grad, gathered, act_hbm, grad_hbm, wg_hbm, wg, sems):
    pairs = ((act0, act_hbm.at[0]), (act1, act_hbm.at[1]), (grad, grad_hbm), (wg, wg_hbm))
    copies = [
        pltpu.make_async_copy(src, dst, sems.at[n]) for n, (src, dst) in enumerate(pairs)
    ]
    for copy in copies[:3]:
        copy.start()

    def tile_rows(tile):
        return gathered[MINE * tile : MINE * tile + MINE]

    for tap in range(9):
        rest = tile_rows(shared_tile(tap))[:, 32 * (tap % 4) : 32 * (tap % 4) + 32]
        first = full_tile(tap)
        window = jnp.concatenate([tile_rows(first), tile_rows(first + 1), rest], axis=1)
        for e in range(3):
            wg[3 * tap + e] = window[:, 96 * e : 96 * e + 96]
    copies[3].start()
    for copy in copies:
        copy.wait()


def channel_order():
    table = np.zeros((COUT, 256), np.float32)
    for r in range(COUT):
        c, rest = divmod(r, HALF)
        block, inside = divmod(rest, 16)
        zz, t = divmod(inside, 2)
        table[r, (2 * zz + c) * MINE + 2 * block + t] = 1.0
    return jnp.asarray(table, BF16)


def per_device(slabs, weight, cotangent):
    any_space = pl.BlockSpec(memory_space=pl.ANY)
    on_chip = pl.BlockSpec(memory_space=pltpu.VMEM)
    in_hbm = pl.BlockSpec(memory_space=pltpu.HBM)
    dma = pltpu.SemaphoreType.DMA

    def held(array):
        return pltpu.with_memory_space_constraint(array, pltpu.VMEM)

    arguments = (
        slabs.reshape(4, 32, LANES),
        weight.reshape(9, 288, COUT),
        cotangent.reshape(2, 16, LANES),
        channel_order(),
    )
    *state, act1 = pl.pallas_call(
        first_kernel,
        out_shape=(
            pltpu.VMEM((32, LANES), BF16),
            pltpu.VMEM((2, 16, LANES), BF16),
            pltpu.VMEM((COUT, 256), BF16),
            pltpu.VMEM((2, 3, 5, 16, LANES + 128), BF16),
            pltpu.VMEM((2, 9, WIN, 256), BF16),
            pltpu.VMEM((2, 128, 256), F32),
            pltpu.VMEM((2, 128, 256), BF16),
            pltpu.VMEM((16, LANES), BF16),
        ),
        in_specs=[in_hbm] * 4,
        out_specs=(on_chip,) * 8,
        scratch_shapes=[
            pltpu.VMEM((4, 32, LANES), BF16),
            pltpu.VMEM((9, 288, COUT), BF16),
            pltpu.VMEM((4, 24, 48, 128), F32),
            pltpu.VMEM((3, 5, 16, LANES + 128), BF16),
            dma((4,)), dma, dma,
        ],
        compiler_params=pltpu.CompilerParams(
            collective_id=0, has_side_effects=True, vmem_limit_bytes=16 << 20
        ),
        name="first_kernel",
    )(*(pltpu.with_memory_space_constraint(array, pltpu.HBM) for array in arguments))
    act0, grad, gathered = pl.pallas_call(
        second_kernel,
        out_shape=(
            pltpu.VMEM((16, LANES), BF16),
            pltpu.VMEM((4, 32, LANES), BF16),
            pltpu.VMEM((16 * PEERS, 128), F32),
        ),
        in_specs=[on_chip] * 7,
        out_specs=(on_chip,) * 3,
        scratch_shapes=[
            pltpu.VMEM((24, 48, 128), F32),
            pltpu.VMEM((3, 1, 16, LANES + 128), BF16),
            pltpu.VMEM((2, 3, 1, 16, LANES + 128), BF16),
            pltpu.VMEM((2, 128, 256), BF16),
            pltpu.VMEM((2, 128, 256), BF16),
            pltpu.VMEM((2, BLOCKS, 16, 128), F32),
            pltpu.VMEM((2, BLOCKS, 16, 128), BF16),
            pltpu.VMEM((BLOCKS, 16, 128), BF16),
            pltpu.VMEM((UNITS, 16, 128), F32),
            pltpu.VMEM((PEERS - 1, UNITS, 16, 128), BF16),
            pltpu.VMEM((PEERS - 1, UNITS, 16, 128), BF16),
            pltpu.VMEM((144, 128), F32),
            pltpu.VMEM((NZ, 24, 128), F32),
            pltpu.VMEM((NZ - 1, 16, 128), F32),
            pltpu.VMEM((4, 24, 40, 128), F32),
            dma, dma, dma((PEERS,)), dma((PEERS,)),
            dma((PEERS - 1,)), dma((PEERS - 1,)), dma((NZ - 1,)), dma((NZ - 1,)),
            dma((PEERS - 1,)), dma((PEERS - 1,)),
        ],
        compiler_params=pltpu.CompilerParams(
            collective_id=1, has_side_effects=True, vmem_limit_bytes=32 << 20
        ),
        name="second_kernel",
    )(*(held(array) for array in state))
    activation, input_grad, gradient = pl.pallas_call(
        hand_over,
        out_shape=(
            jax.ShapeDtypeStruct((2, 16, LANES), BF16),
            jax.ShapeDtypeStruct((4, 32, LANES), BF16),
            jax.ShapeDtypeStruct((27, MINE, 96), F32),
        ),
        in_specs=[on_chip] * 4,
        out_specs=(any_space,) * 3,
        scratch_shapes=[pltpu.VMEM((27, MINE, 96), F32), dma((4,))],
        compiler_params=pltpu.CompilerParams(vmem_limit_bytes=4 << 20),
        name="hand_over",
    )(*(held(array) for array in (act0, act1, grad, gathered)))
    return (
        activation.reshape(1, 2, 16, LANES),
        input_grad.reshape(1, 4, 32, LANES),
        jnp.swapaxes(gradient, 1, 2).reshape(3, 3, 3, 96, MINE),
    )


def solution(mesh):
    placed = (P("sample", "space", None, None), P(), P("sample", "space", None, None))
    return jax.shard_map(
        per_device,
        mesh=mesh,
        in_specs=placed,
        out_specs=(
            P("sample", "space", None, None),
            P("sample", "space", None, None),
            P(None, None, None, None, "space"),
        ),
        check_vma=False,
    )
```
